128 devices in a mesh: heads: 8 (over y, core), seq: 16 (over x, z).
Axes of the slice: x: 4, y: 4, z: 4, core: 2. Of those that a mesh axis runs over, the one named last changes fastest.
Arguments:
- hidden: bfloat16 [2048, 7168], P('seq', 'heads')
- norm_gain: float32 [7168], P('heads'), may hold values from 0.5 to 1.5
- beam_src: int32 [2048], P('seq'), may hold values from 0 to 2047, as said below
- route_ids: int32 [2048, 8], P('seq'), may hold values from 0 to 255, as said below
- route_slots: int32 [2048, 8], P('seq'), may hold values from -1 to 15, as said below
- route_gates: float32 [2048, 8], P('seq'), may hold values from 0.1 to 1
- w_gate: bfloat16 [16, 7168, 2048], P('seq', None, 'heads'), may hold values from -0.0625 to 0.0625
- w_up: bfloat16 [16, 7168, 2048], P('seq', None, 'heads'), may hold values from -0.0625 to 0.0625
- w_down: bfloat16 [16, 2048, 7168], P('seq', 'heads'), may hold values from -0.1875 to 0.1875
- out_grad: bfloat16 [2048, 7168], P('seq', 'heads'), may hold values from -6 to 6
Outputs:
- moe_out: bfloat16 [2048, 7168], P('seq', 'heads')
- grad_hidden: bfloat16 [2048, 7168], P('seq', 'heads')
- grad_gates: float32 [2048, 8], P('seq')
- grad_w_gate: bfloat16 [16, 7168, 2048], P('seq', None, 'heads')
- grad_w_up: bfloat16 [16, 7168, 2048], P('seq', None, 'heads')
- grad_w_down: bfloat16 [16, 2048, 7168], P('seq', 'heads')
The draws below stay inside these ranges and needn't reach their ends.
Inputs may be any that keep to these rules, and one draw needn't show every extreme that they name: beam_src[t] lies in the aligned group of 8 rows that holds t. `route_ids`: each row names 8 different experts of the model's 256; every expert below 16 is named in every aligned block of 128 rows. `route_slots`: in each aligned block of 128 rows, the routes that name one expert e below 16 carry the slots 0 to n - 1, each once, with n at most 16; in every draw one expert below 16 has n = 16 in every block. A route to an expert of 16 or above has slot -1.
All inputs are finite; a program needn't handle non-finite values.
Results may differ from the reference program's by a relative error of at most 0.0073.
Values may be sent and summed in bfloat16 or wider, within the bound.
No kernel may reach another device: no remote copies, remote signals or barrier semaphores. Data moves between devices by JAX's collectives and lax.ppermute only.
A program may use at most 128 MiB of HBM per device.

```python
import math
import jax
import jax.numpy as jnp
from jax import lax

D = 7168
FF = 2048
N_ALL = 256
TOP = 8
BEAM = 8
ROWS = 128
CAP = 8
EXPERTS = 16
TOKENS = 2048
N_SEQ = 16


def block_routes(block_key, lowest, highest):
    key_count, key_order, key_other, key_column = jax.random.split(block_key, 4)
    counts = jax.random.randint(key_count, (EXPERTS,), lowest, highest + 1)
    end_marks = jnp.cumsum(counts)
    start_marks = end_marks - counts
    row_order = jnp.argsort(jax.random.randint(key_order, (ROWS,), 0, 65536) * ROWS + jnp.arange(ROWS, dtype=jnp.int32))
    position = jnp.arange(ROWS, dtype=jnp.int32)[:, None] + ROWS * jnp.arange(TOP, dtype=jnp.int32)[None, :]
    expert = jnp.sum((end_marks[None, None, :] <= position[:, :, None]).astype(jnp.int32), axis=2)
    in_range = position < end_marks[EXPERTS - 1]
    safe_expert = jnp.minimum(expert, EXPERTS - 1)
    slot_pos = position - start_marks[safe_expert]
    candidates = N_ALL - EXPERTS
    scores = jax.random.randint(key_other, (ROWS, candidates), 0, 65536) * candidates + jnp.arange(candidates, dtype=jnp.int32)[None, :]
    others = lax.top_k(scores, TOP)[1].astype(jnp.int32) + EXPERTS
    id_rows = jnp.where(in_range, safe_expert, others)
    slot_rows = jnp.where(in_range, slot_pos, -1)
    column_order = jnp.argsort(jax.random.randint(key_column, (ROWS, TOP), 0, 65536) * TOP + jnp.arange(TOP, dtype=jnp.int32)[None, :], axis=1)
    id_rows = jnp.take_along_axis(id_rows, column_order, axis=1)
    slot_rows = jnp.take_along_axis(slot_rows, column_order, axis=1)
    inverse_order = jnp.argsort(row_order)
    return (id_rows[inverse_order].astype(jnp.int32), slot_rows[inverse_order].astype(jnp.int32))


def routing_tables(key):
    key_star, key_level, key_blocks = jax.random.split(key, 3)
    experts_here = jnp.arange(EXPERTS, dtype=jnp.int32)
    starred = experts_here == jax.random.randint(key_star, (), 0, EXPERTS)
    levels = jax.random.randint(key_level, (EXPERTS,), 1, 5)
    lowest = jnp.where(starred, 2 * CAP, jnp.maximum(levels * CAP // 4, 1))
    highest = jnp.where(starred, 2 * CAP, jnp.maximum(levels * CAP // 2, 1))
    block_keys = jax.random.split(key_blocks, N_SEQ)
    id_blocks, slot_blocks = jax.vmap(block_routes, in_axes=(0, None, None))(block_keys, lowest, highest)
    return (id_blocks.reshape(TOKENS, TOP), slot_blocks.reshape(TOKENS, TOP))


def draw_route_ids(key, part):
    tables = routing_tables(key)
    return tables[0]


def draw_route_slots(key, part):
    tables = routing_tables(key)
    return tables[1]


def draw_beam_src(key, part):
    key = jax.random.fold_in(key, 11)
    offsets = jax.random.randint(key, (TOKENS,), 0, BEAM)
    offsets = offsets.at[0].set(0).at[TOKENS - 1].set(BEAM - 1)
    return (jnp.arange(TOKENS, dtype=jnp.int32) // BEAM * BEAM + offsets).astype(jnp.int32)


def draw_hidden(key, part):
    key = jax.random.fold_in(key, 5)
    key_noise, key_row, key_col = jax.random.split(key, 3)
    trend_line = jnp.exp(0.55 * jnp.arange(D, dtype=jnp.float32) / D)
    noise_field = jax.random.normal(key_noise, (TOKENS, D), jnp.float32)
    row_scale = jnp.exp(jax.random.uniform(key_row, (TOKENS, 1), jnp.float32, -0.7, 1.6))
    col_scale = jnp.exp(jax.random.uniform(key_col, (1, D), jnp.float32, -1.15, 1.15)) * trend_line[None, :]
    return (noise_field * row_scale * col_scale).astype(jnp.bfloat16)


def strengthened(values, key, source, target, parts, factor):
    owner, partner = [(jnp.arange(values.shape[dim]) // (values.shape[dim] // parts)).reshape([-1 if axis == dim else 1 for axis in range(values.ndim)]) for dim in (source, target)]
    chosen = jax.random.permutation(key, parts)[partner]
    strong = (owner == chosen) | (owner == (partner + parts // 2) % parts)
    return jnp.where(strong, factor * values, values)


def block_levels(rng, extent, shards, smallest, largest):
    level, own = 1.0, jax.random.fold_in(rng, 6)
    for dim, shards_of in shards:
        draws = jnp.exp(jax.random.uniform(jax.random.fold_in(own, dim), (shards_of,), jnp.float32, smallest / len(shards), largest / len(shards)))
        level = level * jnp.repeat(draws, extent[dim] // shards_of).reshape([-1 if axis == dim else 1 for axis in range(len(extent))])
    return level


def normal_values(own_key, dims, scale, reach, cuts=(), held_as=jnp.bfloat16):
    result = jax.random.normal(own_key, dims, jnp.float32) * scale
    if len(cuts) > 0:
        result = block_levels(own_key, dims, cuts, -0.22, 0.18) * result
    return jnp.clip(result, min=-reach, max=reach).astype(held_as)


def heavy_noise(key, extent, spread, limit, pieces, heavy, kind=jnp.bfloat16):
    entries = spread * jax.random.normal(key, extent, jnp.float32)
    if pieces:
        entries = entries * block_levels(key, extent, pieces, -0.22, 0.18)
    return jnp.clip(strengthened(entries, jax.random.fold_in(key, 3), *heavy), -limit, limit).astype(kind)


def setup_inputs(seed: int = 0) -> dict:
    key_list = jax.random.split(jax.random.key(seed), 11)
    hidden = draw_hidden(jax.random.fold_in(key_list[10], 71), 0)
    norm_gain = jnp.clip(0.5 + 1.0 * jax.random.uniform(key_list[1], (D,), jnp.float32) ** block_levels(key_list[1], (D,), ((0, 8),), -0.2, 0.2), 0.5, 1.5)
    beam_src = draw_beam_src(jax.random.fold_in(key_list[10], 71), 0)
    route_ids = draw_route_ids(jax.random.fold_in(key_list[10], 71), 0)
    route_slots = draw_route_slots(jax.random.fold_in(key_list[10], 71), 0)
    route_gates = jnp.clip(jnp.exp(math.log(1.0) - 2.3025851 * jax.random.uniform(key_list[5], (TOKENS, TOP), jnp.float32) ** block_levels(key_list[5], (TOKENS, TOP), ((0, 16),), -0.2, 0.2)), 0.1, 1.0)
    w_gate = normal_values(key_list[6], (EXPERTS, D, FF), D ** -0.5, 0.0625, ((0, 16), (2, 8)))
    w_up = normal_values(key_list[7], (EXPERTS, D, FF), D ** -0.5, 0.0625, ((0, 16), (2, 8)))
    w_down = heavy_noise(key_list[8], (EXPERTS, FF, D), FF ** -0.5, 0.1875, ((0, 16), (1, 8)), (1, 2, 8, 2.0))
    out_grad = normal_values(key_list[9], (TOKENS, D), 1.0, 6.0, ((0, 16), (1, 8)))
    return {"hidden": hidden, "norm_gain": norm_gain, "beam_src": beam_src, "route_ids": route_ids, "route_slots": route_slots, "route_gates": route_gates, "w_gate": w_gate, "w_up": w_up, "w_down": w_down, "out_grad": out_grad}


epsilon = 1e-06

def expert_pass(operands):
    expert_in, slot_grad, gate_mat, up_mat, down_mat = operands
    pre_gate = jnp.dot(expert_in, gate_mat, preferred_element_type=jnp.float32)
    pre_up = jnp.dot(expert_in, up_mat, preferred_element_type=jnp.float32)
    sigmoid_gate = jax.nn.sigmoid(pre_gate)
    activated = pre_gate * sigmoid_gate
    hidden_act = (activated * pre_up).astype(jnp.bfloat16)
    expert_out = jnp.dot(hidden_act, down_mat, preferred_element_type=jnp.float32).astype(jnp.bfloat16)
    hid_grad = jnp.dot(slot_grad, down_mat.T, preferred_element_type=jnp.float32)
    grad_down = jnp.dot(hidden_act.T, slot_grad, preferred_element_type=jnp.float32).astype(jnp.bfloat16)
    grad_pre_gate = (hid_grad * pre_up * sigmoid_gate * (1.0 + pre_gate * (1.0 - sigmoid_gate))).astype(jnp.bfloat16)
    grad_pre_up = (hid_grad * activated).astype(jnp.bfloat16)
    grad_gate = jnp.dot(expert_in.T, grad_pre_gate, preferred_element_type=jnp.float32).astype(jnp.bfloat16)
    grad_up = jnp.dot(expert_in.T, grad_pre_up, preferred_element_type=jnp.float32).astype(jnp.bfloat16)
    expert_grad = (jnp.dot(grad_pre_gate, gate_mat.T, preferred_element_type=jnp.float32) + jnp.dot(grad_pre_up, up_mat.T, preferred_element_type=jnp.float32)).astype(jnp.bfloat16)
    return (expert_out, expert_grad, grad_gate, grad_up, grad_down)

def reference(hidden, norm_gain, beam_src, route_ids, route_slots, route_gates, w_gate, w_up, w_down, out_grad):
    token_count = hidden.shape[0]
    expert_count = w_gate.shape[0]
    slot_total = expert_count * N_SEQ * CAP
    beam_rows = hidden[beam_src].astype(jnp.float32)
    inverse = lax.rsqrt(lax.optimization_barrier(jnp.mean(beam_rows * beam_rows, axis=1)) + epsilon)
    normed = (beam_rows * inverse[:, None] * norm_gain[None, :]).astype(jnp.bfloat16)
    block_of = (jnp.arange(token_count, dtype=jnp.int32) // ROWS)[:, None]
    live_route = (route_ids < expert_count) & (route_slots >= 0) & (route_slots < CAP)
    slot_index = jnp.where(live_route, (route_ids * N_SEQ + block_of) * CAP + route_slots, slot_total).astype(jnp.int32)
    owners = jnp.broadcast_to(jnp.arange(token_count, dtype=jnp.int32)[:, None], slot_index.shape)
    source = jnp.full((slot_total + 1,), token_count, jnp.int32).at[slot_index.ravel()].set(owners.ravel())[:slot_total]
    gate_of = jnp.zeros((slot_total + 1,), jnp.float32).at[slot_index.ravel()].set(route_gates.ravel())[:slot_total]
    normed_pad = jnp.concatenate([normed, jnp.zeros((1, D), jnp.bfloat16)], axis=0)
    cot_rows = out_grad.astype(jnp.float32)
    cot_pad = jnp.concatenate([cot_rows, jnp.zeros((1, D), jnp.float32)], axis=0)
    expert_in = normed_pad[source].reshape(expert_count, N_SEQ * CAP, D)
    slot_grad = (gate_of[:, None] * cot_pad[source]).astype(jnp.bfloat16).reshape(expert_count, N_SEQ * CAP, D)
    expert_out, expert_grad, grad_w_gate, grad_w_up, grad_w_down = lax.map(expert_pass, (expert_in, slot_grad, w_gate, w_up, w_down))
    out_flat = jnp.concatenate([expert_out.reshape(slot_total, D), jnp.zeros((1, D), jnp.bfloat16)], axis=0)
    grad_flat = jnp.concatenate([expert_grad.reshape(slot_total, D), jnp.zeros((1, D), jnp.bfloat16)], axis=0)
    moe_acc = jnp.zeros((token_count, D), jnp.float32)
    back_acc = jnp.zeros((token_count, D), jnp.float32)
    gate_cols = []
    for column in range(TOP):
        picked = out_flat[slot_index[:, column]].astype(jnp.float32)
        weight = jnp.where(live_route[:, column], route_gates[:, column], 0.0)
        moe_acc = moe_acc + weight[:, None] * picked
        gate_cols.append(jnp.where(live_route[:, column], lax.optimization_barrier(jnp.sum(cot_rows * picked, axis=1)), 0.0))
        back_acc = back_acc + grad_flat[slot_index[:, column]].astype(jnp.float32)
    moe_out = moe_acc.astype(jnp.bfloat16)
    grad_gates = jnp.stack(gate_cols, axis=1)
    gained = back_acc * norm_gain[None, :]
    gain_dot = lax.optimization_barrier(jnp.sum(gained * beam_rows, axis=1))
    beam_grad = inverse[:, None] * gained - beam_rows * (inverse * inverse * inverse * gain_dot / D)[:, None]
    grad_hidden = jax.ops.segment_sum(beam_grad, beam_src, num_segments=token_count).astype(jnp.bfloat16)
    return (moe_out, grad_hidden, grad_gates, grad_w_gate, grad_w_up, grad_w_down)
```

```python
import jax
import jax.numpy as jnp
from jax import lax
from jax.experimental import pallas as pl
from jax.experimental.pallas import tpu as pltpu
from jax.sharding import Mesh, PartitionSpec as P

D = 7168
CAP = 8
ROWS = 128
FEAT = 896
WIDE = 1024
HID = 256
EPSILON = 1e-06
GATHERED = (0, 3, 1, 2)
HOMEWARD = (0, 1, 3, 2)

f32 = jnp.float32
bf16 = jnp.bfloat16
VMEM = pltpu.VMEM
HBM = "hbm"
RESULT = "result"


def nn(a, b):
    return lax.dot_general(a, b, (((1,), (0,)), ((), ())), preferred_element_type=f32)


def nt(a, b):
    return lax.dot_general(a, b, (((1,), (1,)), ((), ())), preferred_element_type=f32)


def tn(a, b):
    return lax.dot_general(a, b, (((0,), (0,)), ((), ())), preferred_element_type=f32)


def local_call(kernel, inputs, outputs, mib, cost, scalars=0, scratch=()):
    in_specs, args = [], []
    for i, value in enumerate(inputs):
        if i < scalars:
            in_specs.append(pl.BlockSpec(memory_space=pltpu.SMEM))
            args.append(value)
        else:
            in_specs.append(pl.BlockSpec(memory_space=VMEM))
            args.append(pltpu.with_memory_space_constraint(value, VMEM))
    out_shape, out_specs = [], []
    for shape, dtype, space in outputs:
        out_shape.append(space(shape, dtype) if space is VMEM else jax.ShapeDtypeStruct(shape, dtype))
        out_specs.append(pl.BlockSpec(memory_space=pl.ANY if space is HBM else VMEM))
    return pl.pallas_call(
        kernel,
        out_shape=out_shape,
        in_specs=in_specs,
        out_specs=out_specs,
        scratch_shapes=list(scratch),
        compiler_params=pltpu.CompilerParams(vmem_limit_bytes=mib * 2**20),
        cost_estimate=pl.CostEstimate(flops=cost[0], bytes_accessed=cost[1], transcendentals=0),
    )(*args)


def split_two(value):
    high = value.astype(bf16)
    low = (value - high.astype(f32)).astype(bf16)
    return high, low


def slot_matches(ids, slots):
    live = (ids < 16) & (slots >= 0) & (slots < CAP)
    target = jnp.where(live, ids * CAP + slots, ROWS)
    slot = lax.broadcasted_iota(jnp.int32, (ROWS, ROWS), 0)
    return live, [slot == target[k : k + 1, :] for k in range(8)]


def pick_rows(matches, parent):
    pick = matches[0]
    for match in matches[1:]:
        pick = pick | match
    pick = jnp.where(pick, 1.0, 0.0).astype(bf16)
    row = lax.broadcasted_iota(jnp.int32, (ROWS, ROWS), 0)
    from_parent = jnp.where(row == parent, 1.0, 0.0).astype(bf16)
    return pick, nt(pick, from_parent).astype(bf16)


def mix_of(matches, gates):
    mix = jnp.zeros((ROWS, ROWS), f32)
    for k, match in enumerate(matches):
        mix = mix + jnp.where(match, gates[k : k + 1, :], 0.0)
    return mix


def prepare(hidden, gain, source, ids, slots, gates, cotangent, rows_x, rows_g):
    _, matches = slot_matches(ids[...], slots[...])
    pick, select = pick_rows(matches, source[...] & (ROWS - 1))
    gate = jnp.sum(mix_of(matches, gates[...]), axis=1, keepdims=True)
    beam = nn(select, hidden[...])
    rows_x[:, :FEAT] = (beam * gain[...]).astype(bf16)
    square = jnp.sum(beam * beam, axis=1, keepdims=True) * (1.0 / D)
    high, low = split_two(square)
    lane = lax.broadcasted_iota(jnp.int32, (ROWS, WIDE - FEAT), 1)
    tail = jnp.where(lane == 0, high.astype(f32), jnp.where(lane == 1, low.astype(f32), 0.0))
    rows_x[:, FEAT:] = tail.astype(bf16)
    rows_g[...] = (nn(pick, cotangent[...]) * gate).astype(bf16)


def block_of(refs, core, i):
    near, near_other, far, far_other = refs
    if i == 0:
        return (near, near_other)[core]
    return (far[i - 1], far_other.at[i - 1])[core]


def forward(where, x0, s0, x1, x2, x3, s123, w_gate, w_up, w_down, pre_gate, pre_up, act, scale, own, other):
    y, core = where[0], where[1]
    refs = (x0, s0, (x1, x2, x3), s123)
    mean = jnp.zeros((ROWS, WIDE - FEAT), f32)
    gate = jnp.zeros((ROWS, HID), f32)
    up = jnp.zeros((ROWS, HID), f32)
    for side in range(2):
        for i, offset in enumerate(GATHERED):
            block = block_of(refs, side, i)
            head = lax.rem(y + offset, 4) * 2 + (core if side == 0 else 1 - core)
            rows = pl.ds(pl.multiple_of(head * FEAT, FEAT), FEAT)
            mean = mean + block[:, FEAT:].astype(f32)
            gate = gate + nn(block[:, :FEAT], w_gate[0, rows, :])
            up = up + nn(block[:, :FEAT], w_up[0, rows, :])
    inverse = lax.rsqrt(jnp.sum(mean, axis=1, keepdims=True) + EPSILON)
    gate = gate * inverse
    up = up * inverse
    hidden_act = (gate * jax.nn.sigmoid(gate) * up).astype(bf16)
    pre_gate[...] = gate
    pre_up[...] = up
    act[...] = hidden_act
    scale[...] = jnp.broadcast_to(inverse, (ROWS, 128))
    for side, result in ((1, other), (0, own)):
        for i, offset in enumerate(HOMEWARD):
            head = lax.rem(y + offset, 4) * 2 + (core if side == 0 else 1 - core)
            columns = pl.ds(pl.multiple_of(head * FEAT, 128), FEAT)
            result[i] = nn(hidden_act, w_down[0, :, columns]).astype(bf16)


def backward(
    where, g0, s0, g1, g2, g3, s123, w_gate, w_up, w_down, pre_gate, pre_up, act, scale, grad_gate, grad_up, own, other
):
    y, core = where[0], where[1]
    refs = (g0, s0, (g1, g2, g3), s123)
    hid = jnp.zeros((ROWS, HID), f32)
    for side in range(2):
        for i, offset in enumerate(GATHERED):
            block = block_of(refs, side, i)
            head = lax.rem(y + offset, 4) * 2 + (core if side == 0 else 1 - core)
            columns = pl.ds(pl.multiple_of(head * FEAT, 128), FEAT)
            hid = hid + nt(block[...], w_down[0, :, columns])
    gate, up = pre_gate[...], pre_up[...]
    inverse = scale[:, 0:1]
    sigmoid = jax.nn.sigmoid(gate)
    score = jnp.sum(act[...].astype(f32) * hid, axis=1, keepdims=True)
    scaled = hid * inverse
    d_gate = (scaled * up * sigmoid * (1.0 + gate * (1.0 - sigmoid))).astype(bf16)
    d_up = (scaled * gate * sigmoid).astype(bf16)
    grad_gate[...] = d_gate
    grad_up[...] = d_up
    dot = jnp.sum(d_gate.astype(f32) * gate + d_up.astype(f32) * up, axis=1, keepdims=True)
    dot = dot * inverse * (1.0 / D)
    lane = lax.broadcasted_iota(jnp.int32, (ROWS, WIDE - FEAT), 1)
    me = 2 * (y * 2 + core)
    tail = jnp.zeros((ROWS, WIDE - FEAT), f32)
    for base, value in ((0, score), (64, dot)):
        high, low = split_two(value)
        tail = jnp.where(lane == base + me, high.astype(f32), tail)
        tail = jnp.where(lane == base + me + 1, low.astype(f32), tail)
    tail = tail.astype(bf16)
    for side, result in ((1, other), (0, own)):
        for i, offset in enumerate(HOMEWARD):
            head = lax.rem(y + offset, 4) * 2 + (core if side == 0 else 1 - core)
            rows = pl.ds(pl.multiple_of(head * FEAT, FEAT), FEAT)
            term = nt(d_gate, w_gate[0, rows, :]) + nt(d_up, w_up[0, rows, :])
            result[i, :, :FEAT] = term.astype(bf16)
            result[i, :, FEAT:] = tail


def weight_grads(
    where, x0, xs0, x1, x2, x3, xs123, g0, gs0, g1, g2, g3, gs123, act, grad_gate, grad_up,
    out_gate, out_up, out_down, buf_gate, buf_up, buf_down, sems,
):
    y, core = where[0], where[1]
    x_refs = (x0, xs0, (x1, x2, x3), xs123)
    g_refs = (g0, gs0, (g1, g2, g3), gs123)
    act_t = act[...].T
    pending = {}
    for n in range(8):
        side, i = divmod(n, 4)
        slot = n % 2
        head = lax.rem(y + GATHERED[i], 4) * 2 + (core if side == 0 else 1 - core)
        rows = pl.ds(pl.multiple_of(head * FEAT, FEAT), FEAT)
        columns = pl.ds(pl.multiple_of(head * FEAT, 128), FEAT)
        if slot in pending:
            for copy in pending[slot]:
                copy.wait()
        x_t = block_of(x_refs, side, i)[:, :FEAT].T
        buf_gate[slot] = nn(x_t, grad_gate[...]).astype(bf16)
        buf_up[slot] = nn(x_t, grad_up[...]).astype(bf16)
        buf_down[slot] = nn(act_t, block_of(g_refs, side, i)[...]).astype(bf16)
        pending[slot] = [
            pltpu.make_async_copy(buf_gate.at[slot], out_gate.at[0, rows, :], sems.at[slot, 0]),
            pltpu.make_async_copy(buf_up.at[slot], out_up.at[0, rows, :], sems.at[slot, 1]),
            pltpu.make_async_copy(buf_down.at[slot], out_down.at[0, :, columns], sems.at[slot, 2]),
        ]
        for copy in pending[slot]:
            copy.start()
    for copies in pending.values():
        for copy in copies:
            copy.wait()


def finish(out_rows, in_rows, hidden, gain, source, ids, slots, gates, moe, grad_hidden, grad_gates):
    live, matches = slot_matches(ids[...], slots[...])
    _, select = pick_rows(matches, source[...] & (ROWS - 1))
    mix = mix_of(matches, gates[...])
    first = mix.astype(bf16)
    rest = mix - first.astype(f32)
    second = rest.astype(bf16)
    third = (rest - second.astype(f32)).astype(bf16)
    rows = out_rows[...]
    moe[...] = (tn(first, rows) + (tn(second, rows) + tn(third, rows))).astype(bf16)
    tail = in_rows[:, FEAT:].astype(f32)
    lane = lax.broadcasted_iota(jnp.int32, tail.shape, 1)
    score = jnp.sum(jnp.where(lane < 64, tail, 0.0), axis=1, keepdims=True)
    dot = jnp.sum(jnp.where(lane < 64, 0.0, tail), axis=1, keepdims=True)
    found = [jnp.sum(jnp.where(match, score, 0.0), axis=0, keepdims=True) for match in matches]
    found = jnp.concatenate(found, axis=0)
    grad_gates[...] = jnp.where(live, found / gates[...], 0.0)
    back = tn(select, in_rows[:, :FEAT]) * gain[...]
    dots = jnp.where(select.astype(f32) > 0, dot, 0.0)
    per_parent = jnp.sum(dots.T, axis=1, keepdims=True)
    grad_hidden[...] = (back - hidden[...].astype(f32) * per_parent).astype(bf16)


def to_y(values, step):
    return lax.ppermute(values, "y", [(i, (i + step) % 4) for i in range(4)])


def to_sibling(values):
    return lax.ppermute(values, "core", [(0, 1), (1, 0)])


def gather(block):
    sibling = to_sibling(block)
    far = [to_y(block, 1), to_y(block, 3), to_y(block, 2)]
    return (block, sibling, *far, to_sibling(jnp.stack(far)))


def send_home(own, other):
    received = to_sibling(other)
    total = (own.astype(f32) + received.astype(f32)).astype(bf16)
    parts = [to_y(total[1], 1), to_y(total[2], 3), to_y(total[3], 2)]
    summed = total[0].astype(f32)
    for part in parts:
        summed = summed + part.astype(f32)
    return summed.astype(bf16)


def exchange(rows):
    width = rows.shape[1]
    pieces = rows.reshape(16, CAP, width)
    return lax.all_to_all(pieces, ("x", "z"), 0, 0, tiled=True).reshape(ROWS, width)


def on_device(
    hidden, norm_gain, beam_src, route_ids, route_slots, route_gates, w_gate, w_up, w_down, out_grad
):
    where = jnp.stack([lax.axis_index("y"), lax.axis_index("core")]).astype(jnp.int32)
    gain = norm_gain.reshape(1, FEAT)
    source = beam_src.reshape(1, ROWS)
    ids, slots, gates = route_ids.T, route_slots.T, route_gates.T
    rows_x, rows_g = local_call(
        prepare,
        (hidden, gain, source, ids, slots, gates, out_grad),
        [((ROWS, WIDE), bf16, VMEM), ((ROWS, FEAT), bf16, VMEM)],
        8,
        (10**8, 10**6),
    )
    sent = exchange(jnp.concatenate([rows_x, rows_g], axis=1))
    x_blocks = gather(sent[:, :WIDE])
    g_blocks = gather(sent[:, WIDE:])
    pre_gate, pre_up, act, scale, out_own, out_other = local_call(
        forward,
        (where, *x_blocks, w_gate, w_up, w_down),
        [
            ((ROWS, HID), f32, VMEM),
            ((ROWS, HID), f32, VMEM),
            ((ROWS, HID), bf16, VMEM),
            ((ROWS, 128), f32, VMEM),
            ((4, ROWS, FEAT), bf16, VMEM),
            ((4, ROWS, FEAT), bf16, VMEM),
        ],
        8,
        (3 * 2 * ROWS * D * HID, 10**6),
        scalars=1,
    )
    out_rows = send_home(out_own, out_other)
    d_gate, d_up, in_own, in_other = local_call(
        backward,
        (where, *g_blocks, w_gate, w_up, w_down, pre_gate, pre_up, act, scale),
        [
            ((ROWS, HID), bf16, VMEM),
            ((ROWS, HID), bf16, VMEM),
            ((4, ROWS, WIDE), bf16, VMEM),
            ((4, ROWS, WIDE), bf16, VMEM),
        ],
        8,
        (3 * 2 * ROWS * D * HID, 10**6),
        scalars=1,
    )
    in_rows = send_home(in_own, in_other)
    grads = local_call(
        weight_grads,
        (where, *x_blocks, *g_blocks, act, d_gate, d_up),
        [((1, D, HID), bf16, HBM), ((1, D, HID), bf16, HBM), ((1, HID, D), bf16, HBM)],
        16,
        (2 * 3 * 2 * ROWS * D * HID, 11 * 10**6),
        scalars=1,
        scratch=(
            VMEM((2, FEAT, HID), bf16),
            VMEM((2, FEAT, HID), bf16),
            VMEM((2, HID, FEAT), bf16),
            pltpu.SemaphoreType.DMA((2, 3)),
        ),
    )
    home = exchange(jnp.concatenate([out_rows, in_rows], axis=1))
    moe, grad_hidden, grad_gates = local_call(
        finish,
        (home[:, :FEAT], home[:, FEAT:], hidden, gain, source, ids, slots, gates),
        [((ROWS, FEAT), bf16, RESULT), ((ROWS, FEAT), bf16, RESULT), ((8, ROWS), f32, RESULT)],
        8,
        (10**8, 10**6),
    )
    return (moe, grad_hidden, grad_gates.T, *grads)


def solution(mesh):
    split = Mesh(mesh.devices.reshape(4, 2, 4, 4), ("y", "core", "x", "z"))
    heads, seq = ("y", "core"), ("x", "z")
    return jax.shard_map(
        on_device,
        mesh=split,
        in_specs=(
            P(seq, heads),
            P(heads),
            P(seq),
            P(seq, None),
            P(seq, None),
            P(seq, None),
            P(seq, None, heads),
            P(seq, None, heads),
            P(seq, heads, None),
            P(seq, heads),
        ),
        out_specs=(
            P(seq, heads),
            P(seq, heads),
            P(seq, None),
            P(seq, None, heads),
            P(seq, None, heads),
            P(seq, heads, None),
        ),
        check_vma=False,
    )
```

```python
import jax
import jax.numpy as jnp
from jax import lax
from jax.experimental import pallas as pl
from jax.experimental.pallas import tpu as pltpu
from jax.sharding import Mesh, PartitionSpec as P

D = 7168
CAP = 8
ROWS = 128
FEAT = 896
WIDE = 1024
HID = 256
EPSILON = 1e-06
GATHERED = (0, 3, 1, 2)
HOMEWARD = (0, 1, 3, 2)

f32 = jnp.float32
bf16 = jnp.bfloat16
SMEM, VMEM, COPY, HBM = "smem", "vmem", "copy", "hbm"


def nn(a, b):
    return lax.dot_general(a, b, (((1,), (0,)), ((), ())), preferred_element_type=f32)


def nt(a, b):
    return lax.dot_general(a, b, (((1,), (1,)), ((), ())), preferred_element_type=f32)


def tn(a, b):
    return lax.dot_general(a, b, (((0,), (0,)), ((), ())), preferred_element_type=f32)


def local_call(kernel, inputs, outputs, mib, cost, scratch=()):
    in_specs, args = [], []
    for kind, value in inputs:
        space = {SMEM: pltpu.SMEM, HBM: pl.ANY}.get(kind, pltpu.VMEM)
        in_specs.append(pl.BlockSpec(memory_space=space))
        if kind != SMEM:
            value = pltpu.with_memory_space_constraint(value, pltpu.VMEM if kind == VMEM else pltpu.HBM)
        args.append(value)
    out_shape, out_specs = [], []
    for kind, shape, dtype in outputs:
        space = {VMEM: pltpu.VMEM, HBM: pltpu.HBM}.get(kind, jax.ShapeDtypeStruct)
        out_shape.append(space(shape, dtype))
        out_specs.append(pl.BlockSpec(memory_space=pl.ANY if kind == HBM else pltpu.VMEM))
    return pl.pallas_call(
        kernel,
        out_shape=out_shape,
        in_specs=in_specs,
        out_specs=out_specs,
        scratch_shapes=list(scratch),
        compiler_params=pltpu.CompilerParams(vmem_limit_bytes=mib * 2**20),
        cost_estimate=pl.CostEstimate(flops=cost[0], bytes_accessed=cost[1], transcendentals=0),
    )(*args)


def held(*values):
    return [(VMEM, value) for value in values]


def fetched(*values):
    return [(COPY, value) for value in values]


def split_two(value):
    high = value.astype(bf16)
    low = (value - high.astype(f32)).astype(bf16)
    return high, low


def slot_matches(ids, slots):
    live = (ids < 16) & (slots >= 0) & (slots < CAP)
    target = jnp.where(live, ids * CAP + slots, ROWS)
    slot = lax.broadcasted_iota(jnp.int32, (ROWS, ROWS), 0)
    return live, [slot == target[k : k + 1, :] for k in range(8)]


def pick_rows(matches, parent):
    pick = matches[0]
    for match in matches[1:]:
        pick = pick | match
    pick = jnp.where(pick, 1.0, 0.0).astype(bf16)
    row = lax.broadcasted_iota(jnp.int32, (ROWS, ROWS), 0)
    from_parent = jnp.where(row == parent, 1.0, 0.0).astype(bf16)
    return pick, nt(pick, from_parent).astype(bf16)


def mix_of(matches, gates):
    mix = jnp.zeros((ROWS, ROWS), f32)
    for k, match in enumerate(matches):
        mix = mix + jnp.where(match, gates[k : k + 1, :], 0.0)
    return mix


def prepare(hidden, gain, source, ids, slots, gates, cotangent, rows, kept):
    _, matches = slot_matches(ids[...], slots[...])
    pick, select = pick_rows(matches, source[...] & (ROWS - 1))
    gate = jnp.sum(mix_of(matches, gates[...]), axis=1, keepdims=True)
    beam = nn(select, hidden[...])
    rows[:, :FEAT] = (beam * gain[...][None, :]).astype(bf16)
    square = jnp.sum(beam * beam, axis=1, keepdims=True) * (1.0 / D)
    high, low = split_two(square)
    lane = lax.broadcasted_iota(jnp.int32, (ROWS, WIDE - FEAT), 1)
    tail = jnp.where(lane == 0, high.astype(f32), jnp.where(lane == 1, low.astype(f32), 0.0))
    rows[:, FEAT:WIDE] = tail.astype(bf16)
    rows[:, WIDE:] = (nn(pick, cotangent[...]) * gate).astype(bf16)
    kept[...] = hidden[...]


def turn_weights(gate, up, down, gate_t, up_t, down_t, wide, tall, wide_t, tall_t, sems):
    loads = [
        pltpu.make_async_copy(down, tall, sems.at[0]),
        pltpu.make_async_copy(gate, wide.at[0], sems.at[1]),
        pltpu.make_async_copy(up, wide.at[1], sems.at[2]),
    ]
    stores = [
        pltpu.make_async_copy(tall_t, down_t, sems.at[3]),
        pltpu.make_async_copy(wide_t.at[0], gate_t, sems.at[4]),
        pltpu.make_async_copy(wide_t.at[1], up_t, sems.at[5]),
    ]
    for load in loads:
        load.start()
    loads[0].wait()
    for head in range(8):
        part = slice(head * FEAT, (head + 1) * FEAT)
        tall_t[part, :] = tall[0, :, part].T
    stores[0].start()
    for i in range(2):
        loads[1 + i].wait()
        for head in range(8):
            part = slice(head * FEAT, (head + 1) * FEAT)
            wide_t[i, :, part] = wide[i, 0, part, :].T
        stores[1 + i].start()
    for store in stores:
        store.wait()


def head_at(where, offset, side):
    core = where[1] if side == 0 else 1 - where[1]
    return lax.rem(where[0] + offset, 4) * 2 + core


def row_part(head):
    return pl.ds(pl.multiple_of(head * FEAT, FEAT), FEAT)


def column_part(head):
    return pl.ds(pl.multiple_of(head * FEAT, 128), FEAT)


def forward(where, *refs):
    blocks, weights, (pre_gate, pre_up, act, scale) = refs[:8], refs[8:11], refs[11:15]
    own, other, (w_gate, w_up, w_down, sems) = refs[15:19], refs[19:23], refs[23:]
    loads = [
        pltpu.make_async_copy(source, target, sems.at[i])
        for i, (source, target) in enumerate(zip(weights, (w_gate, w_up, w_down)))
    ]
    for load in loads:
        load.start()
    mean = jnp.zeros((ROWS, WIDE - FEAT), f32)
    for block in blocks:
        mean = mean + block[:, FEAT:WIDE].astype(f32)
    pre = []
    for load, weight in zip(loads, (w_gate, w_up)):
        load.wait()
        total = jnp.zeros((ROWS, HID), f32)
        for n, block in enumerate(blocks):
            rows = row_part(head_at(where, GATHERED[n % 4], n // 4))
            total = total + nn(block[:, :FEAT], weight[0, rows, :])
        pre.append(total)
    gate, up = pre
    inverse = lax.rsqrt(jnp.sum(mean, axis=1, keepdims=True) + EPSILON)
    gate = gate * inverse
    up = up * inverse
    hidden_act = (gate * jax.nn.sigmoid(gate) * up).astype(bf16)
    pre_gate[...] = gate
    pre_up[...] = up
    act[...] = hidden_act
    scale[...] = jnp.broadcast_to(inverse, (ROWS, 128))
    loads[2].wait()
    for side, result in ((1, other), (0, own)):
        for i, offset in enumerate(HOMEWARD):
            columns = column_part(head_at(where, offset, side))
            result[i][...] = nn(hidden_act, w_down[0, :, columns]).astype(bf16)


def backward(where, *refs):
    blocks = refs[:8]
    gate_t, up_t, down_t, pre_gate, pre_up, act, scale, grad_gate, grad_up = refs[8:17]
    own, other = refs[17:21], refs[21:25]
    hid = jnp.zeros((ROWS, HID), f32)
    for n, block in enumerate(blocks):
        hid = hid + nn(g_part(block)[...], down_t[row_part(head_at(where, GATHERED[n % 4], n // 4)), :])
    gate, up = pre_gate[...], pre_up[...]
    inverse = scale[:, 0:1]
    sigmoid = jax.nn.sigmoid(gate)
    score = jnp.sum(act[...].astype(f32) * hid, axis=1, keepdims=True)
    scaled = hid * inverse
    d_gate = (scaled * up * sigmoid * (1.0 + gate * (1.0 - sigmoid))).astype(bf16)
    d_up = (scaled * gate * sigmoid).astype(bf16)
    grad_gate[...] = d_gate
    grad_up[...] = d_up
    dot = jnp.sum(d_gate.astype(f32) * gate + d_up.astype(f32) * up, axis=1, keepdims=True)
    dot = dot * inverse * (1.0 / D)
    lane = lax.broadcasted_iota(jnp.int32, (ROWS, WIDE - FEAT), 1)
    me = 2 * head_at(where, 0, 0)
    tail = jnp.zeros((ROWS, WIDE - FEAT), f32)
    for base, value in ((0, score), (64, dot)):
        high, low = split_two(value)
        tail = jnp.where(lane == base + me, high.astype(f32), tail)
        tail = jnp.where(lane == base + me + 1, low.astype(f32), tail)
    tail = tail.astype(bf16)
    for side, result in ((1, other), (0, own)):
        for i, offset in enumerate(HOMEWARD):
            columns = column_part(head_at(where, offset, side))
            term = nn(d_gate, gate_t[:, columns]) + nn(d_up, up_t[:, columns])
            result[i][:, :FEAT] = term.astype(bf16)
            result[i][:, FEAT:] = tail


def weight_grads(where, *refs):
    x_blocks = refs[:8]
    g_blocks = (refs[0], *refs[8:11], refs[4], *refs[11:14])
    act, grad_gate, grad_up, out_gate, out_up, out_down, buf_gate, buf_up, buf_down, sems = refs[14:]
    act_t = act[...].T
    pending = {}
    for n in range(8):
        slot = n % 2
        head = head_at(where, GATHERED[n % 4], n // 4)
        for copy in pending.get(slot, ()):
            copy.wait()
        x_t = x_blocks[n][:, :FEAT].T
        buf_gate[slot] = nn(x_t, grad_gate[...]).astype(bf16)
        buf_up[slot] = nn(x_t, grad_up[...]).astype(bf16)
        buf_down[slot] = nn(act_t, g_part(g_blocks[n])[...]).astype(bf16)
        pending[slot] = [
            pltpu.make_async_copy(buf_gate.at[slot], out_gate.at[0, row_part(head), :], sems.at[slot, 0]),
            pltpu.make_async_copy(buf_up.at[slot], out_up.at[0, row_part(head), :], sems.at[slot, 1]),
            pltpu.make_async_copy(buf_down.at[slot], out_down.at[0, :, column_part(head)], sems.at[slot, 2]),
        ]
        for copy in pending[slot]:
            copy.start()
    for copies in pending.values():
        for copy in copies:
            copy.wait()


def finish(home, hidden, gain, source, ids, slots, gates, moe, grad_hidden, grad_gates):
    live, matches = slot_matches(ids[...], slots[...])
    _, select = pick_rows(matches, source[...] & (ROWS - 1))
    mix = mix_of(matches, gates[...])
    first = mix.astype(bf16)
    rest = mix - first.astype(f32)
    second = rest.astype(bf16)
    third = (rest - second.astype(f32)).astype(bf16)
    rows = home[:, :FEAT]
    moe[...] = (tn(first, rows) + (tn(second, rows) + tn(third, rows))).astype(bf16)
    tail = home[:, FEAT + FEAT :].astype(f32)
    lane = lax.broadcasted_iota(jnp.int32, tail.shape, 1)
    score = jnp.sum(jnp.where(lane < 64, tail, 0.0), axis=1, keepdims=True)
    dot = jnp.sum(jnp.where(lane < 64, 0.0, tail), axis=1, keepdims=True)
    found = [jnp.sum(jnp.where(match, score, 0.0), axis=0, keepdims=True) for match in matches]
    found = jnp.concatenate(found, axis=0)
    grad_gates[...] = jnp.where(live, found / gates[...], 0.0)
    back = tn(select, home[:, FEAT : FEAT + FEAT]) * gain[...][None, :]
    dots = jnp.where(select.astype(f32) > 0, dot, 0.0)
    per_parent = jnp.sum(dots.T, axis=1, keepdims=True)
    grad_hidden[...] = (back - hidden[...].astype(f32) * per_parent).astype(bf16)


def to_y(values, step):
    return lax.ppermute(values, "y", [(i, (i + step) % 4) for i in range(4)])


def to_sibling(values):
    return lax.ppermute(values, "core", [(0, 1), (1, 0)])


def gather(sent, sibling, part):
    block = sent[:, part]
    far = [to_y(block, 1), to_y(block, 3), to_y(block, 2)]
    return [sent, *far, sibling, *[to_sibling(value) for value in far]]


def g_part(block):
    return block if block.shape[1] == FEAT else block.at[:, WIDE:]


def chip_sums(own, other):
    return [(mine.astype(f32) + to_sibling(theirs).astype(f32)).astype(bf16) for mine, theirs in zip(own, other)]


def sent_home(sums):
    return [to_y(sums[1], 1), to_y(sums[2], 3), to_y(sums[3], 2)]


def row_sum(mine, parts):
    total = mine.astype(f32)
    for part in parts:
        total = total + part.astype(f32)
    return total.astype(bf16)


def exchange(rows):
    width = rows.shape[1]
    pieces = rows.reshape(16, CAP, width)
    return lax.all_to_all(pieces, ("x", "z"), 0, 0, tiled=True).reshape(ROWS, width)


def on_device(
    hidden, norm_gain, beam_src, route_ids, route_slots, route_gates, w_gate, w_up, w_down, out_grad
):
    where = (SMEM, jnp.stack([lax.axis_index("y"), lax.axis_index("core")]).astype(jnp.int32))
    gain = norm_gain
    source = beam_src.reshape(1, ROWS)
    ids, slots, gates = route_ids.T, route_slots.T, route_gates.T
    rows, kept = local_call(
        prepare,
        fetched(hidden, gain, source, ids, slots, gates, out_grad),
        [(VMEM, (ROWS, WIDE + FEAT), bf16), (VMEM, (ROWS, FEAT), bf16)],
        8,
        (0, 1000),
    )
    turned = local_call(
        turn_weights,
        [(HBM, w_gate), (HBM, w_up), (HBM, w_down)],
        [(HBM, (HID, D), bf16), (HBM, (HID, D), bf16), (HBM, (D, HID), bf16)],
        24,
        (0, 60 * 10**6),
        scratch=(
            pltpu.VMEM((2, 1, D, HID), bf16),
            pltpu.VMEM((1, HID, D), bf16),
            pltpu.VMEM((2, HID, D), bf16),
            pltpu.VMEM((D, HID), bf16),
            pltpu.SemaphoreType.DMA((6,)),
        ),
    )
    sent = exchange(rows)
    sent, *turned = lax.optimization_barrier((sent, *turned))
    sibling = to_sibling(sent)
    x_blocks = gather(sent, sibling, slice(None, WIDE))
    g_blocks = gather(sent, sibling, slice(WIDE, None))
    pre_gate, pre_up, act, scale, *out_terms = local_call(
        forward,
        [where, *held(*x_blocks), (HBM, w_gate), (HBM, w_up), (HBM, w_down)],
        [
            (VMEM, (ROWS, HID), f32),
            (VMEM, (ROWS, HID), f32),
            (VMEM, (ROWS, HID), bf16),
            (VMEM, (ROWS, 128), f32),
            *[(VMEM, (ROWS, FEAT), bf16)] * 8,
        ],
        16,
        (10**10, 1000),
        scratch=(
            pltpu.VMEM((1, D, HID), bf16),
            pltpu.VMEM((1, D, HID), bf16),
            pltpu.VMEM((1, HID, D), bf16),
            pltpu.SemaphoreType.DMA((3,)),
        ),
    )
    out_sums = chip_sums(out_terms[:4], out_terms[4:])
    out_parts = sent_home(out_sums)
    d_gate, d_up, *in_terms = local_call(
        backward,
        [where, *held(*g_blocks, *turned, pre_gate, pre_up, act, scale)],
        [
            (VMEM, (ROWS, HID), bf16),
            (VMEM, (ROWS, HID), bf16),
            *[(VMEM, (ROWS, WIDE), bf16)] * 8,
        ],
        4,
        (10**10, 1000),
    )
    in_terms, out_parts = lax.optimization_barrier((in_terms, out_parts))
    in_sums = chip_sums(in_terms[:4], in_terms[4:])
    out_rows = row_sum(out_sums[0], out_parts)
    in_rows = row_sum(in_sums[0], sent_home(in_sums))
    grads = local_call(
        weight_grads,
        [where, *fetched(*x_blocks, *g_blocks[1:4], *g_blocks[5:], act, d_gate, d_up)],
        [(HBM, (1, D, HID), bf16), (HBM, (1, D, HID), bf16), (HBM, (1, HID, D), bf16)],
        12,
        (2 * 3 * 2 * ROWS * D * HID, 22 * 10**6),
        scratch=(
            pltpu.VMEM((2, FEAT, HID), bf16),
            pltpu.VMEM((2, FEAT, HID), bf16),
            pltpu.VMEM((2, HID, FEAT), bf16),
            pltpu.SemaphoreType.DMA((2, 3)),
        ),
    )
    home = exchange(jnp.concatenate([out_rows, in_rows], axis=1))
    moe, grad_hidden, grad_gates = local_call(
        finish,
        held(home, kept) + fetched(gain, source, ids, slots, gates),
        [(COPY, (ROWS, FEAT), bf16), (COPY, (ROWS, FEAT), bf16), (COPY, (8, ROWS), f32)],
        8,
        (0, 1000),
    )
    return (moe, grad_hidden, grad_gates.T, *grads)


def solution(mesh):
    split = Mesh(mesh.devices.reshape(4, 2, 4, 4), ("y", "core", "x", "z"))
    heads, seq = ("y", "core"), ("x", "z")
    return jax.shard_map(
        on_device,
        mesh=split,
        in_specs=(
            P(seq, heads),
            P(heads),
            P(seq),
            P(seq, None),
            P(seq, None),
            P(seq, None),
            P(seq, None, heads),
            P(seq, None, heads),
            P(seq, heads, None),
            P(seq, heads),
        ),
        out_specs=(
            P(seq, heads),
            P(seq, heads),
            P(seq, None),
            P(seq, None, heads),
            P(seq, None, heads),
            P(seq, heads, None),
        ),
        check_vma=False,
    )
```

```python
import jax
import jax.numpy as jnp
from jax import lax
from jax.experimental import pallas as pl
from jax.experimental.pallas import tpu as pltpu
from jax.sharding import Mesh, PartitionSpec as P

D = 7168
CAP = 8
ROWS = 128
FEAT = 896
WIDE = 1024
BOTH = WIDE + FEAT
HID = 256
EPSILON = 1e-06
OFFSETS = (0, 1, 3, 2)
HALF = ROWS // 2

f32 = jnp.float32
bf16 = jnp.bfloat16
SMEM, VMEM, COPY, HBM = "smem", "vmem", "copy", "hbm"


def nn(a, b):
    return lax.dot_general(a, b, (((1,), (0,)), ((), ())), preferred_element_type=f32)


def nt(a, b):
    return lax.dot_general(a, b, (((1,), (1,)), ((), ())), preferred_element_type=f32)


def tn(a, b):
    return lax.dot_general(a, b, (((0,), (0,)), ((), ())), preferred_element_type=f32)


def local_call(kernel, inputs, outputs, mib, cost, scratch=()):
    in_specs, args = [], []
    for kind, value in inputs:
        space = {SMEM: pltpu.SMEM, HBM: pl.ANY}.get(kind, pltpu.VMEM)
        in_specs.append(pl.BlockSpec(memory_space=space))
        if kind != SMEM:
            value = pltpu.with_memory_space_constraint(value, pltpu.VMEM if kind == VMEM else pltpu.HBM)
        args.append(value)
    out_shape, out_specs = [], []
    for kind, shape, dtype in outputs:
        space = {VMEM: pltpu.VMEM, HBM: pltpu.HBM}.get(kind, jax.ShapeDtypeStruct)
        out_shape.append(space(shape, dtype))
        out_specs.append(pl.BlockSpec(memory_space=pl.ANY if kind == HBM else pltpu.VMEM))
    return pl.pallas_call(
        kernel,
        out_shape=out_shape,
        in_specs=in_specs,
        out_specs=out_specs,
        scratch_shapes=list(scratch),
        compiler_params=pltpu.CompilerParams(vmem_limit_bytes=mib * 2**20),
        cost_estimate=pl.CostEstimate(flops=cost[0], bytes_accessed=cost[1], transcendentals=0),
    )(*args)


def held(*values):
    return [(VMEM, value) for value in values]


def fetched(*values):
    return [(COPY, value) for value in values]


def split_two(value):
    high = value.astype(bf16)
    low = (value - high.astype(f32)).astype(bf16)
    return high, low


def slot_matches(ids, slots):
    live = (ids < 16) & (slots >= 0) & (slots < CAP)
    target = jnp.where(live, ids * CAP + slots, ROWS)
    slot = lax.broadcasted_iota(jnp.int32, (ROWS, ROWS), 0)
    return live, [slot == target[k : k + 1, :] for k in range(8)]


def pick_rows(matches, parent):
    pick = matches[0]
    for match in matches[1:]:
        pick = pick | match
    pick = jnp.where(pick, 1.0, 0.0).astype(bf16)
    row = lax.broadcasted_iota(jnp.int32, (ROWS, ROWS), 0)
    from_parent = jnp.where(row == parent, 1.0, 0.0).astype(bf16)
    return pick, nt(pick, from_parent).astype(bf16)


def mix_of(matches, gates):
    mix = jnp.zeros((ROWS, ROWS), f32)
    for k, match in enumerate(matches):
        mix = mix + jnp.where(match, gates[k : k + 1, :], 0.0)
    return mix


def prepare(hidden, gain, source, ids, slots, gates, cotangent, rows, kept):
    _, matches = slot_matches(ids[...], slots[...])
    pick, select = pick_rows(matches, source[...] & (ROWS - 1))
    gate = jnp.sum(mix_of(matches, gates[...]), axis=1, keepdims=True)
    beam = nn(select, hidden[...])
    rows[:, :FEAT] = (beam * gain[...][None, :]).astype(bf16)
    square = jnp.sum(beam * beam, axis=1, keepdims=True) * (1.0 / D)
    high, low = split_two(square)
    lane = lax.broadcasted_iota(jnp.int32, (ROWS, WIDE - FEAT), 1)
    tail = jnp.where(lane == 0, high.astype(f32), jnp.where(lane == 1, low.astype(f32), 0.0))
    rows[:, FEAT:WIDE] = tail.astype(bf16)
    rows[:, WIDE:] = (nn(pick, cotangent[...]) * gate).astype(bf16)
    kept[...] = hidden[...]


def turn_weights(gate, up, down, gate_t, up_t, down_t, wide, tall, wide_t, tall_t, sems):
    loads = [
        pltpu.make_async_copy(down, tall, sems.at[0]),
        pltpu.make_async_copy(gate, wide.at[0], sems.at[1]),
        pltpu.make_async_copy(up, wide.at[1], sems.at[2]),
    ]
    stores = [
        pltpu.make_async_copy(tall_t, down_t, sems.at[3]),
        pltpu.make_async_copy(wide_t.at[0], gate_t, sems.at[4]),
        pltpu.make_async_copy(wide_t.at[1], up_t, sems.at[5]),
    ]
    for load in loads:
        load.start()
    loads[0].wait()
    for head in range(8):
        part = slice(head * FEAT, (head + 1) * FEAT)
        tall_t[part, :] = tall[0, :, part].T
    stores[0].start()
    for i in range(2):
        loads[1 + i].wait()
        for head in range(8):
            part = slice(head * FEAT, (head + 1) * FEAT)
            wide_t[i, :, part] = wide[i, 0, part, :].T
        stores[1 + i].start()
    for store in stores:
        store.wait()


def head_at(where, offset, side):
    core = where[1] if side == 0 else 1 - where[1]
    return lax.rem(where[0] + offset, 4) * 2 + core


def row_part(head):
    return pl.ds(pl.multiple_of(head * FEAT, FEAT), FEAT)


def column_part(head):
    return pl.ds(pl.multiple_of(head * FEAT, 128), FEAT)


def first_blocks(where, *refs):
    blocks, (w_gate, w_up, w_down_t) = refs[:6], refs[6:9]
    gate, up, hid, mean, late_gate, late_up, late_down = refs[9:16]
    rows_gate, rows_up, rows_down, sems = refs[16:]
    loads, late = [], []
    for n in range(8):
        side, i = divmod(n, 4)
        head = head_at(where, OFFSETS[i], side)
        part = row_part(head)
        for j, (source, early, later) in enumerate(
            (
                (w_gate.at[0], rows_gate, late_gate),
                (w_up.at[0], rows_up, late_up),
                (w_down_t, rows_down, late_down),
            )
        ):
            target = later.at[side] if i == 3 else early.at[3 * side + i]
            copy = pltpu.make_async_copy(source.at[part, :], target, sems.at[n, j])
            (late if i == 3 else loads).append(copy)
    for copy in loads + late:
        copy.start()
    totals = [jnp.zeros((ROWS, HID), f32) for _ in range(3)]
    squares = jnp.zeros((ROWS, WIDE - FEAT), f32)
    for n, block in enumerate(blocks):
        squares = squares + block[:, FEAT:WIDE].astype(f32)
        for j, weight in enumerate((rows_gate, rows_up, rows_down)):
            loads[3 * n + j].wait()
            columns = slice(0, FEAT) if j < 2 else slice(WIDE, BOTH)
            totals[j] = totals[j] + nn(block[:, columns], weight[n])
    for copy in late:
        copy.wait()
    gate[...], up[...], hid[...] = totals
    mean[...] = squares


def expert_terms(where, act, d_gate, d_up, w_down, gate_t, up_t, side, results, tail):
    for i in (3, 1, 2, 0):
        columns = column_part(head_at(where, OFFSETS[i], side))
        results[i][:, :FEAT] = nn(act, w_down[0, :, columns]).astype(bf16)
        term = nn(d_gate, gate_t[:, columns]) + nn(d_up, up_t[:, columns])
        results[i][:, FEAT : FEAT + FEAT] = term.astype(bf16)
        results[i][:, FEAT + FEAT :] = tail


def last_blocks(where, *refs):
    halves, (late_gate, late_up, late_down) = refs[:4], refs[4:7]
    first_gate, first_up, first_hid, mean, w_down, gate_t, up_t = refs[7:14]
    act, grad_gate, grad_up, tail_out, *other = refs[14:]
    gate, up, hid = first_gate[...], first_up[...], first_hid[...]
    squares = mean[...]
    for side in range(2):
        block = jnp.concatenate([halves[2 * side][...], halves[2 * side + 1][...]], axis=0)
        squares = squares + block[:, FEAT:WIDE].astype(f32)
        gate = gate + nn(block[:, :FEAT], late_gate[side])
        up = up + nn(block[:, :FEAT], late_up[side])
        hid = hid + nn(block[:, WIDE:], late_down[side])
    inverse = lax.rsqrt(jnp.sum(squares, axis=1, keepdims=True) + EPSILON)
    gate = gate * inverse
    up = up * inverse
    sigmoid = jax.nn.sigmoid(gate)
    hidden_act = (gate * sigmoid * up).astype(bf16)
    score = jnp.sum(hidden_act.astype(f32) * hid, axis=1, keepdims=True)
    scaled = hid * inverse
    d_gate = (scaled * up * sigmoid * (1.0 + gate * (1.0 - sigmoid))).astype(bf16)
    d_up = (scaled * gate * sigmoid).astype(bf16)
    act[...] = hidden_act
    grad_gate[...] = d_gate
    grad_up[...] = d_up
    dot = jnp.sum(d_gate.astype(f32) * gate + d_up.astype(f32) * up, axis=1, keepdims=True)
    dot = dot * inverse * (1.0 / D)
    lane = lax.broadcasted_iota(jnp.int32, (ROWS, WIDE - FEAT), 1)
    me = 2 * head_at(where, 0, 0)
    tail = jnp.zeros((ROWS, WIDE - FEAT), f32)
    for base, value in ((0, score), (64, dot)):
        high, low = split_two(value)
        tail = jnp.where(lane == base + me, high.astype(f32), tail)
        tail = jnp.where(lane == base + me + 1, low.astype(f32), tail)
    tail = tail.astype(bf16)
    tail_out[...] = tail
    expert_terms(where, hidden_act, d_gate, d_up, w_down, gate_t, up_t, 1, other, tail)


def own_terms(where, act, grad_gate, grad_up, tail, w_down, gate_t, up_t, *own):
    expert_terms(where, act[...], grad_gate[...], grad_up[...], w_down, gate_t, up_t, 0, own, tail[...])


def weight_grads(where, *refs):
    blocks = refs[:3], refs[3:5], refs[5:8], refs[8:10]
    act, grad_gate, grad_up, out_gate, out_up, out_down, buf_gate, buf_up, buf_down, sems = refs[10:]
    act_t = act[...].T
    pending = {}
    for n in range(8):
        side, i = divmod(n, 4)
        slot = n % 2
        head = head_at(where, OFFSETS[i], side)
        for copy in pending.get(slot, ()):
            copy.wait()
        if i < 3:
            block = blocks[2 * side][i][...]
        else:
            block = jnp.concatenate([half[...] for half in blocks[2 * side + 1]], axis=0)
        beam_t = block[:, :FEAT].T
        buf_gate[slot] = nn(beam_t, grad_gate[...]).astype(bf16)
        buf_up[slot] = nn(beam_t, grad_up[...]).astype(bf16)
        buf_down[slot] = nn(act_t, block[:, WIDE:]).astype(bf16)
        pending[slot] = [
            pltpu.make_async_copy(buf_gate.at[slot], out_gate.at[0, row_part(head), :], sems.at[slot, 0]),
            pltpu.make_async_copy(buf_up.at[slot], out_up.at[0, row_part(head), :], sems.at[slot, 1]),
            pltpu.make_async_copy(buf_down.at[slot], out_down.at[0, :, column_part(head)], sems.at[slot, 2]),
        ]
        for copy in pending[slot]:
            copy.start()
    for copies in pending.values():
        for copy in copies:
            copy.wait()


def finish(home, hidden, gain, source, ids, slots, gates, moe, grad_hidden, grad_gates):
    live, matches = slot_matches(ids[...], slots[...])
    _, select = pick_rows(matches, source[...] & (ROWS - 1))
    mix = mix_of(matches, gates[...])
    first = mix.astype(bf16)
    rest = mix - first.astype(f32)
    second = rest.astype(bf16)
    third = (rest - second.astype(f32)).astype(bf16)
    rows = home[:, :FEAT]
    moe[...] = (tn(first, rows) + (tn(second, rows) + tn(third, rows))).astype(bf16)
    tail = home[:, FEAT + FEAT :].astype(f32)
    lane = lax.broadcasted_iota(jnp.int32, tail.shape, 1)
    score = jnp.sum(jnp.where(lane < 64, tail, 0.0), axis=1, keepdims=True)
    dot = jnp.sum(jnp.where(lane < 64, 0.0, tail), axis=1, keepdims=True)
    found = [jnp.sum(jnp.where(match, score, 0.0), axis=0, keepdims=True) for match in matches]
    found = jnp.concatenate(found, axis=0)
    grad_gates[...] = jnp.where(live, found / gates[...], 0.0)
    back = tn(select, home[:, FEAT : FEAT + FEAT]) * gain[...][None, :]
    dots = jnp.where(select.astype(f32) > 0, dot, 0.0)
    per_parent = jnp.sum(dots.T, axis=1, keepdims=True)
    grad_hidden[...] = (back - hidden[...].astype(f32) * per_parent).astype(bf16)


def to_y(values, step):
    return lax.ppermute(values, "y", [(i, (i + step) % 4) for i in range(4)])


def to_sibling(values):
    return lax.ppermute(values, "core", [(0, 1), (1, 0)])


def sent_home(sums):
    mine, above, below, across = sums
    for_above, for_below = to_y(across[:HALF], 1), to_y(across[HALF:], 3)
    above = joined(above, jnp.pad(for_above, ((0, HALF), (0, 0))))
    below = joined(below, jnp.pad(for_below, ((HALF, 0), (0, 0))))
    return joined(mine, to_y(above, 1), to_y(below, 3))


def joined(*parts):
    total = parts[0].astype(f32)
    for part in parts[1:]:
        total = total + part.astype(f32)
    return total.astype(bf16)


def exchange(rows):
    width = rows.shape[1]
    pieces = rows.reshape(16, CAP, width)
    return lax.all_to_all(pieces, ("x", "z"), 0, 0, tiled=True).reshape(ROWS, width)


def on_device(
    hidden, norm_gain, beam_src, route_ids, route_slots, route_gates, w_gate, w_up, w_down, out_grad
):
    where = (SMEM, jnp.stack([lax.axis_index("y"), lax.axis_index("core")]).astype(jnp.int32))
    gain = norm_gain
    source = beam_src.reshape(1, ROWS)
    ids, slots, gates = route_ids.T, route_slots.T, route_gates.T
    rows, kept = local_call(
        prepare,
        fetched(hidden, gain, source, ids, slots, gates, out_grad),
        [(VMEM, (ROWS, WIDE + FEAT), bf16), (VMEM, (ROWS, FEAT), bf16)],
        8,
        (0, 1000),
    )
    turned = local_call(
        turn_weights,
        [(HBM, w_gate), (HBM, w_up), (HBM, w_down)],
        [(HBM, (HID, D), bf16), (HBM, (HID, D), bf16), (HBM, (D, HID), bf16)],
        24,
        (0, 60 * 10**6),
        scratch=(
            pltpu.VMEM((2, 1, D, HID), bf16),
            pltpu.VMEM((1, HID, D), bf16),
            pltpu.VMEM((2, HID, D), bf16),
            pltpu.VMEM((D, HID), bf16),
            pltpu.SemaphoreType.DMA((6,)),
        ),
    )
    sent = exchange(rows)
    above, below = to_y(sent, 3), to_y(sent, 1)
    above, below, gate_t, up_t, down_t = lax.optimization_barrier((above, below, *turned))
    across = [to_y(below[:HALF], 1), to_y(above[HALF:], 3)]
    near = [sent, above, below]
    near_sibling = [to_sibling(value) for value in near]
    gate, up, hid, mean, *late = local_call(
        first_blocks,
        [where, *held(*near, *near_sibling), (HBM, w_gate), (HBM, w_up), (HBM, down_t)],
        [
            *[(VMEM, (ROWS, HID), f32)] * 3,
            (VMEM, (ROWS, WIDE - FEAT), f32),
            *[(VMEM, (2, FEAT, HID), bf16)] * 3,
        ],
        16,
        (10**10, 1000),
        scratch=(*[pltpu.VMEM((6, FEAT, HID), bf16)] * 3, pltpu.SemaphoreType.DMA((8, 3))),
    )
    across, mean = lax.optimization_barrier((across, mean))
    across_sibling = [to_sibling(value) for value in across]
    act, d_gate, d_up, tail, *other = local_call(
        last_blocks,
        [where, *held(*across, *across_sibling, *late, gate, up, hid, mean, w_down, gate_t, up_t)],
        [
            *[(VMEM, (ROWS, HID), bf16)] * 3,
            (VMEM, (ROWS, WIDE - FEAT), bf16),
            *[(VMEM, (ROWS, BOTH), bf16)] * 4,
        ],
        4,
        (10**9, 1000),
    )
    theirs = [to_sibling(value) for value in other]
    own = local_call(
        own_terms,
        [where, *held(act, d_gate, d_up, tail, w_down, gate_t, up_t)],
        [(VMEM, (ROWS, BOTH), bf16)] * 4,
        4,
        (2 * 10**9, 1000),
    )
    grads = local_call(
        weight_grads,
        [where, *fetched(*near, *across, *near_sibling, *across_sibling, act, d_gate, d_up)],
        [(HBM, (1, D, HID), bf16), (HBM, (1, D, HID), bf16), (HBM, (1, HID, D), bf16)],
        12,
        (2 * 3 * 2 * ROWS * D * HID, 22 * 10**6),
        scratch=(
            pltpu.VMEM((2, FEAT, HID), bf16),
            pltpu.VMEM((2, FEAT, HID), bf16),
            pltpu.VMEM((2, HID, FEAT), bf16),
            pltpu.SemaphoreType.DMA((2, 3)),
        ),
    )
    home_sums = sent_home([joined(mine, term) for mine, term in zip(own, theirs)])
    home_sums, *grads = lax.optimization_barrier((home_sums, *grads))
    home = exchange(home_sums)
    moe, grad_hidden, grad_gates = local_call(
        finish,
        held(home, kept) + fetched(gain, source, ids, slots, gates),
        [(COPY, (ROWS, FEAT), bf16), (COPY, (ROWS, FEAT), bf16), (COPY, (8, ROWS), f32)],
        8,
        (0, 1000),
    )
    return (moe, grad_hidden, grad_gates.T, *grads)


def solution(mesh):
    split = Mesh(mesh.devices.reshape(4, 2, 4, 4), ("y", "core", "x", "z"))
    heads, seq = ("y", "core"), ("x", "z")
    return jax.shard_map(
        on_device,
        mesh=split,
        in_specs=(
            P(seq, heads),
            P(heads),
            P(seq),
            P(seq, None),
            P(seq, None),
            P(seq, None),
            P(seq, None, heads),
            P(seq, None, heads),
            P(seq, heads, None),
            P(seq, heads),
        ),
        out_specs=(
            P(seq, heads),
            P(seq, heads),
            P(seq, None),
            P(seq, None, heads),
            P(seq, None, heads),
            P(seq, heads, None),
        ),
        check_vma=False,
    )
```

```python
import jax
import jax.numpy as jnp
from jax import lax
from jax.experimental import pallas as pl
from jax.experimental.pallas import tpu as pltpu
from jax.sharding import Mesh, PartitionSpec as P

D = 7168
CAP = 8
ROWS = 128
FEAT = 896
WIDE = 1024
BOTH = WIDE + FEAT
HID = 256
EPSILON = 1e-06
PLACES = ((0, 1, 3, 2), (0, 3, 1, 2))

f32 = jnp.float32
bf16 = jnp.bfloat16
SMEM, VMEM, COPY, HBM = "smem", "vmem", "copy", "hbm"


def nn(a, b):
    return lax.dot_general(a, b, (((1,), (0,)), ((), ())), preferred_element_type=f32)


def nt(a, b):
    return lax.dot_general(a, b, (((1,), (1,)), ((), ())), preferred_element_type=f32)


def tn(a, b):
    return lax.dot_general(a, b, (((0,), (0,)), ((), ())), preferred_element_type=f32)


def local_call(kernel, inputs, outputs, mib, cost, scratch=()):
    in_specs, args = [], []
    for kind, value in inputs:
        space = {SMEM: pltpu.SMEM, HBM: pl.ANY}.get(kind, pltpu.VMEM)
        in_specs.append(pl.BlockSpec(memory_space=space))
        if kind != SMEM:
            value = pltpu.with_memory_space_constraint(value, pltpu.VMEM if kind == VMEM else pltpu.HBM)
        args.append(value)
    out_shape, out_specs = [], []
    for kind, shape, dtype in outputs:
        space = {VMEM: pltpu.VMEM, HBM: pltpu.HBM}.get(kind, jax.ShapeDtypeStruct)
        out_shape.append(space(shape, dtype))
        out_specs.append(pl.BlockSpec(memory_space=pl.ANY if kind == HBM else pltpu.VMEM))
    return pl.pallas_call(
        kernel,
        out_shape=out_shape,
        in_specs=in_specs,
        out_specs=out_specs,
        scratch_shapes=list(scratch),
        compiler_params=pltpu.CompilerParams(vmem_limit_bytes=mib * 2**20),
        cost_estimate=pl.CostEstimate(flops=cost[0], bytes_accessed=cost[1], transcendentals=0),
    )(*args)


def held(*values):
    return [(VMEM, value) for value in values]


def fetched(*values):
    return [(COPY, value) for value in values]


def split_two(value):
    high = value.astype(bf16)
    low = (value - high.astype(f32)).astype(bf16)
    return high, low


def slot_matches(ids, slots):
    live = (ids < 16) & (slots >= 0) & (slots < CAP)
    target = jnp.where(live, ids * CAP + slots, ROWS)
    slot = lax.broadcasted_iota(jnp.int32, (ROWS, ROWS), 0)
    return live, [slot == target[k : k + 1, :] for k in range(8)]


def pick_rows(matches, parent):
    pick = matches[0]
    for match in matches[1:]:
        pick = pick | match
    pick = jnp.where(pick, 1.0, 0.0).astype(bf16)
    row = lax.broadcasted_iota(jnp.int32, (ROWS, ROWS), 0)
    from_parent = jnp.where(row == parent, 1.0, 0.0).astype(bf16)
    return pick, nt(pick, from_parent).astype(bf16)


def mix_of(matches, gates):
    mix = jnp.zeros((ROWS, ROWS), f32)
    for k, match in enumerate(matches):
        mix = mix + jnp.where(match, gates[k : k + 1, :], 0.0)
    return mix


def prepare(hidden, gain, source, ids, slots, gates, cotangent, rows, kept):
    _, matches = slot_matches(ids[...], slots[...])
    pick, select = pick_rows(matches, source[...] & (ROWS - 1))
    gate = jnp.sum(mix_of(matches, gates[...]), axis=1, keepdims=True)
    beam = nn(select, hidden[...])
    rows[:, :FEAT] = (beam * gain[...][None, :]).astype(bf16)
    square = jnp.sum(beam * beam, axis=1, keepdims=True) * (1.0 / D)
    high, low = split_two(square)
    lane = lax.broadcasted_iota(jnp.int32, (ROWS, WIDE - FEAT), 1)
    tail = jnp.where(lane == 0, high.astype(f32), jnp.where(lane == 1, low.astype(f32), 0.0))
    rows[:, FEAT:WIDE] = tail.astype(bf16)
    rows[:, WIDE:] = (nn(pick, cotangent[...]) * gate).astype(bf16)
    kept[...] = hidden[...]


def turn_weights(gate, up, gate_t, up_t, wide, wide_t, sems):
    loads = [pltpu.make_async_copy(source, wide.at[i], sems.at[i]) for i, source in enumerate((gate, up))]
    stores = [pltpu.make_async_copy(wide_t.at[i], target, sems.at[2 + i]) for i, target in enumerate((gate_t, up_t))]
    for load in loads:
        load.start()
    for i in range(2):
        loads[i].wait()
        for head in range(8):
            part = slice(head * FEAT, (head + 1) * FEAT)
            wide_t[i, :, part] = wide[i, 0, part, :].T
        stores[i].start()
    for store in stores:
        store.wait()


def heads_here():
    y, core = lax.axis_index("y"), lax.axis_index("core")
    heads = []
    for side in (core, 1 - core):
        heads += [(y ^ jnp.where(side == 0, PLACES[0][i], PLACES[1][i])) * 2 + side for i in range(4)]
    return jnp.stack(heads).astype(jnp.int32)


def head_at(heads, place, side):
    return heads[4 * side + place]


def row_part(head):
    return pl.ds(pl.multiple_of(head * FEAT, FEAT), FEAT)


def column_part(head):
    return pl.ds(pl.multiple_of(head * FEAT, 128), FEAT)


def weight_copies(where, side, place, weights, targets, sems):
    head = head_at(where, place, side)
    w_gate, w_up, w_down = weights
    sources = (w_gate.at[0, row_part(head), :], w_up.at[0, row_part(head), :], w_down.at[0, :, column_part(head)])
    copies = [pltpu.make_async_copy(*pair, sems.at[j]) for j, pair in enumerate(zip(sources, targets))]
    for copy in copies:
        copy.start()
    return copies


def add_blocks(copies, blocks, parts, totals, squares):
    gate, up, hid = totals
    for n, block in enumerate(blocks):
        squares = squares + block[:, FEAT:WIDE].astype(f32)
        for copy in copies[n]:
            copy.wait()
        gate = gate + nn(block[:, :FEAT], parts[0][n])
        up = up + nn(block[:, :FEAT], parts[1][n])
        hid = hid + nt(block[:, WIDE:], parts[2][n])
    return (gate, up, hid), squares


def own_blocks(where, own, sibling, w_gate, w_up, w_down, *refs):
    gate, up, hid, mean, late_gate, late_up, late_down, *parts, late, sems = refs
    weights = (w_gate, w_up, w_down)
    copies = [weight_copies(where, side, 0, weights, [p.at[side] for p in parts], sems.at[side]) for side in range(2)]
    last = [
        weight_copies(where, side, 3, weights, (late_gate.at[side], late_up.at[side], late.at[side]), sems.at[2 + side])
        for side in range(2)
    ]
    zero = jnp.zeros((ROWS, HID), f32)
    squares = jnp.zeros((ROWS, WIDE - FEAT), f32)
    totals, squares = add_blocks(copies, (own, sibling), parts, (zero, zero, zero), squares)
    for side in range(2):
        for copy in last[side]:
            copy.wait()
        late_down[side] = late[side].T
    gate[...], up[...], hid[...] = totals
    mean[...] = squares


def near_blocks(where, *refs):
    blocks, weights, sums, results, (*parts, sems) = refs[:4], refs[4:7], refs[7:11], refs[11:15], refs[15:]
    places = ((0, 1), (0, 2), (1, 1), (1, 2))
    copies = [
        weight_copies(where, side, place, weights, [p.at[n] for p in parts], sems.at[n])
        for n, (side, place) in enumerate(places)
    ]
    totals, squares = add_blocks(copies, blocks, parts, [ref[...] for ref in sums[:3]], sums[3][...])
    results[0][...], results[1][...], results[2][...] = totals
    results[3][...] = squares


def expert_terms(where, act, d_gate, d_up, w_down, gate_t, up_t, side, results, tail):
    for i in (3, 1, 2, 0):
        columns = column_part(head_at(where, i, side))
        results[i][:, :FEAT] = nn(act, w_down[0, :, columns]).astype(bf16)
        term = nn(d_gate, gate_t[:, columns]) + nn(d_up, up_t[:, columns])
        results[i][:, FEAT : FEAT + FEAT] = term.astype(bf16)
        results[i][:, FEAT + FEAT :] = tail


def last_blocks(where, *refs):
    blocks, (late_gate, late_up, late_down) = refs[:2], refs[2:5]
    first_gate, first_up, first_hid, mean, w_down, gate_t, up_t = refs[5:12]
    act, grad_gate, grad_up, tail_out, *other = refs[12:]
    gate, up, hid = first_gate[...], first_up[...], first_hid[...]
    squares = mean[...]
    for side, block in enumerate(blocks):
        squares = squares + block[:, FEAT:WIDE].astype(f32)
        gate = gate + nn(block[:, :FEAT], late_gate[side])
        up = up + nn(block[:, :FEAT], late_up[side])
        hid = hid + nn(block[:, WIDE:], late_down[side])
    inverse = lax.rsqrt(jnp.sum(squares, axis=1, keepdims=True) + EPSILON)
    gate = gate * inverse
    up = up * inverse
    sigmoid = jax.nn.sigmoid(gate)
    hidden_act = (gate * sigmoid * up).astype(bf16)
    score = jnp.sum(hidden_act.astype(f32) * hid, axis=1, keepdims=True)
    scaled = hid * inverse
    d_gate = (scaled * up * sigmoid * (1.0 + gate * (1.0 - sigmoid))).astype(bf16)
    d_up = (scaled * gate * sigmoid).astype(bf16)
    act[...] = hidden_act
    grad_gate[...] = d_gate
    grad_up[...] = d_up
    dot = jnp.sum(d_gate.astype(f32) * gate + d_up.astype(f32) * up, axis=1, keepdims=True)
    dot = dot * inverse * (1.0 / D)
    lane = lax.broadcasted_iota(jnp.int32, (ROWS, WIDE - FEAT), 1)
    me = 2 * head_at(where, 0, 0)
    tail = jnp.zeros((ROWS, WIDE - FEAT), f32)
    for base, value in ((0, score), (64, dot)):
        high, low = split_two(value)
        tail = jnp.where(lane == base + me, high.astype(f32), tail)
        tail = jnp.where(lane == base + me + 1, low.astype(f32), tail)
    tail = tail.astype(bf16)
    tail_out[...] = tail
    expert_terms(where, hidden_act, d_gate, d_up, w_down, gate_t, up_t, 1, other, tail)


def own_terms(where, act, grad_gate, grad_up, tail, w_down, gate_t, up_t, *own):
    expert_terms(where, act[...], grad_gate[...], grad_up[...], w_down, gate_t, up_t, 0, own, tail[...])


def weight_grads(where, *refs):
    blocks, (act, grad_gate, grad_up, out_gate, out_up, out_down) = refs[:8], refs[8:14]
    held_rows, buf_gate, buf_up, buf_down, load_sems, store_sems = refs[14:]
    loads = [pltpu.make_async_copy(block, held_rows.at[n], load_sems.at[n]) for n, block in enumerate(blocks)]
    for load in loads:
        load.start()
    act_t = act[...].T
    stores = []
    for n in range(8):
        loads[n].wait()
        head = head_at(where, n % 4, n // 4)
        beam_t = held_rows[n, :, :FEAT].T
        for j, (left, right, buf, target) in enumerate(
            (
                (act_t, held_rows[n, :, WIDE:], buf_down, out_down.at[0, :, column_part(head)]),
                (beam_t, grad_gate[...], buf_gate, out_gate.at[0, row_part(head), :]),
                (beam_t, grad_up[...], buf_up, out_up.at[0, row_part(head), :]),
            )
        ):
            buf[n] = nn(left, right).astype(bf16)
            stores.append(pltpu.make_async_copy(buf.at[n], target, store_sems.at[n, j]))
            stores[-1].start()
    for store in stores:
        store.wait()


def route_tables(ids, slots, gates, source, gain, select, mix, targets, kept_gates, kept_gain):
    live, matches = slot_matches(ids[...], slots[...])
    select[...] = pick_rows(matches, source[...] & (ROWS - 1))[1]
    rest = mix_of(matches, gates[...])
    for i in range(3):
        mix[i] = rest.astype(bf16)
        rest = rest - mix[i].astype(f32)
    targets[...] = jnp.where(live, ids[...] * CAP + slots[...], ROWS)
    kept_gates[...] = gates[...]
    kept_gain[...] = gain[...][None, :]


def finish(home, hidden, select, mix, targets, gates, gain, moe, grad_hidden, grad_gates):
    rows = home[:, :FEAT]
    moe[...] = (tn(mix[0], rows) + (tn(mix[1], rows) + tn(mix[2], rows))).astype(bf16)
    tail = home[:, FEAT + FEAT :].astype(f32)
    lane = lax.broadcasted_iota(jnp.int32, tail.shape, 1)
    score = jnp.sum(jnp.where(lane < 64, tail, 0.0), axis=1, keepdims=True)
    dot = jnp.sum(jnp.where(lane < 64, 0.0, tail), axis=1, keepdims=True)
    slot = lax.broadcasted_iota(jnp.int32, (ROWS, ROWS), 0)
    found = [
        jnp.sum(jnp.where(slot == targets[k : k + 1, :], score, 0.0), axis=0, keepdims=True) for k in range(8)
    ]
    found = jnp.concatenate(found, axis=0)
    grad_gates[...] = jnp.where(targets[...] < ROWS, found / gates[...], 0.0)
    picks = select[...]
    back = tn(picks, home[:, FEAT : FEAT + FEAT]) * gain[...]
    dots = jnp.where(picks.astype(f32) > 0, dot, 0.0)
    per_parent = jnp.sum(dots.T, axis=1, keepdims=True)
    grad_hidden[...] = (back - hidden[...].astype(f32) * per_parent).astype(bf16)


def to_place(values, place):
    pairs = [(2 * y + core, 2 * (y ^ PLACES[core][place]) + core) for y in range(4) for core in range(2)]
    return lax.ppermute(values, ("y", "core"), pairs)


def to_sibling(values):
    return lax.ppermute(values, "core", [(0, 1), (1, 0)])


def sent_home(sums, beside):
    mine, first, second, across = sums
    passing, beside = lax.optimization_barrier((to_place(across, 2), beside))
    first = joined(first, passing)
    return joined(mine, to_place(first, 1), to_place(second, 2)), beside


def joined(*parts):
    total = parts[0].astype(f32)
    for part in parts[1:]:
        total = total + part.astype(f32)
    return total.astype(bf16)


def exchange(rows):
    width = rows.shape[1]
    pieces = rows.reshape(16, CAP, width)
    return lax.all_to_all(pieces, ("x", "z"), 0, 0, tiled=True).reshape(ROWS, width)


def on_device(
    hidden, norm_gain, beam_src, route_ids, route_slots, route_gates, w_gate, w_up, w_down, out_grad
):
    where = (SMEM, heads_here())
    gain = norm_gain
    source = beam_src.reshape(1, ROWS)
    ids, slots, gates = route_ids.T, route_slots.T, route_gates.T
    rows, kept = local_call(
        prepare,
        fetched(hidden, gain, source, ids, slots, gates, out_grad),
        [(VMEM, (ROWS, WIDE + FEAT), bf16), (VMEM, (ROWS, FEAT), bf16)],
        8,
        (0, 1000),
    )
    turned = local_call(
        turn_weights,
        [(HBM, w_gate), (HBM, w_up)],
        [(HBM, (HID, D), bf16), (HBM, (HID, D), bf16)],
        20,
        (0, 60 * 10**6),
        scratch=(
            pltpu.VMEM((2, 1, D, HID), bf16),
            pltpu.VMEM((2, HID, D), bf16),
            pltpu.SemaphoreType.DMA((4,)),
        ),
    )
    sent = exchange(rows)
    weights = [(HBM, w_gate), (HBM, w_up), (HBM, w_down)]
    sums = [*[(VMEM, (ROWS, HID), f32)] * 3, (VMEM, (ROWS, WIDE - FEAT), f32)]
    sibling = to_sibling(sent)
    *early, late_gate, late_up, late_down = local_call(
        own_blocks,
        [where, *held(sent, sibling), *weights],
        [*sums, *[(VMEM, (2, FEAT, HID), bf16)] * 3],
        8,
        (0, 1000),
        scratch=(
            pltpu.VMEM((2, FEAT, HID), bf16),
            pltpu.VMEM((2, FEAT, HID), bf16),
            pltpu.VMEM((2, HID, FEAT), bf16),
            pltpu.VMEM((2, HID, FEAT), bf16),
            pltpu.SemaphoreType.DMA((4, 3)),
        ),
    )
    first, second = to_place(sent, 1), to_place(sent, 2)
    first, second, gate_t, up_t, *early = lax.optimization_barrier((first, second, *turned, *early))
    across = to_place(first, 2)
    near = [sent, first, second]
    near_sibling = [sibling, to_sibling(first), to_sibling(second)]
    gate, up, hid, mean = local_call(
        near_blocks,
        [where, *held(*near[1:], *near_sibling[1:]), *weights, *held(*early)],
        sums,
        12,
        (10**10, 1000),
        scratch=(
            pltpu.VMEM((4, FEAT, HID), bf16),
            pltpu.VMEM((4, FEAT, HID), bf16),
            pltpu.VMEM((4, HID, FEAT), bf16),
            pltpu.SemaphoreType.DMA((4, 3)),
        ),
    )
    across, mean = lax.optimization_barrier((across, mean))
    across_sibling = to_sibling(across)
    act, d_gate, d_up, tail, *other = local_call(
        last_blocks,
        [where, *held(across, across_sibling, late_gate, late_up, late_down, gate, up, hid, mean, w_down, gate_t, up_t)],
        [
            *[(VMEM, (ROWS, HID), bf16)] * 3,
            (VMEM, (ROWS, WIDE - FEAT), bf16),
            *[(VMEM, (ROWS, BOTH), bf16)] * 4,
        ],
        4,
        (10**9, 1000),
    )
    theirs = [to_sibling(value) for value in other]
    own = local_call(
        own_terms,
        [where, *held(act, d_gate, d_up, tail, w_down, gate_t, up_t)],
        [(VMEM, (ROWS, BOTH), bf16)] * 4,
        4,
        (2 * 10**9, 1000),
    )
    blocks = [(HBM, block) for block in (*near, across, *near_sibling, across_sibling)]
    home_sums = [joined(mine, term) for mine, term in zip(own, theirs)]
    home_sums[3], late_gates = lax.optimization_barrier((home_sums[3], gates))
    tables = local_call(
        route_tables,
        fetched(ids, slots, late_gates, source, gain),
        [
            (VMEM, (ROWS, ROWS), bf16),
            (VMEM, (3, ROWS, ROWS), bf16),
            (VMEM, (8, ROWS), jnp.int32),
            (VMEM, (8, ROWS), f32),
            (VMEM, (1, FEAT), f32),
        ],
        4,
        (0, 1000),
    )
    home_sums, tables = sent_home(home_sums, tables)
    grads = local_call(
        weight_grads,
        [where, *blocks, *fetched(act, d_gate, d_up)],
        [(HBM, (1, D, HID), bf16), (HBM, (1, D, HID), bf16), (HBM, (1, HID, D), bf16)],
        20,
        (2 * 3 * 2 * ROWS * D * HID, 22 * 10**6),
        scratch=(
            pltpu.VMEM((8, ROWS, BOTH), bf16),
            pltpu.VMEM((8, FEAT, HID), bf16),
            pltpu.VMEM((8, FEAT, HID), bf16),
            pltpu.VMEM((8, HID, FEAT), bf16),
            pltpu.SemaphoreType.DMA((8,)),
            pltpu.SemaphoreType.DMA((8, 3)),
        ),
    )
    home_sums, *grads = lax.optimization_barrier((home_sums, *grads))
    home = exchange(home_sums)
    moe, grad_hidden, grad_gates = local_call(
        finish,
        held(home, kept, *tables),
        [(COPY, (ROWS, FEAT), bf16), (COPY, (ROWS, FEAT), bf16), (COPY, (8, ROWS), f32)],
        4,
        (0, 1000),
    )
    return (moe, grad_hidden, grad_gates.T, *grads)


def solution(mesh):
    split = Mesh(mesh.devices.reshape(4, 2, 4, 4), ("y", "core", "x", "z"))
    heads, seq = ("y", "core"), ("x", "z")
    return jax.shard_map(
        on_device,
        mesh=split,
        in_specs=(
            P(seq, heads),
            P(heads),
            P(seq),
            P(seq, None),
            P(seq, None),
            P(seq, None),
            P(seq, None, heads),
            P(seq, None, heads),
            P(seq, heads, None),
            P(seq, heads),
        ),
        out_specs=(
            P(seq, heads),
            P(seq, heads),
            P(seq, None),
            P(seq, None, heads),
            P(seq, None, heads),
            P(seq, heads, None),
        ),
        check_vma=False,
    )
```

```python
import jax
import jax.numpy as jnp
from jax import lax
from jax.experimental import pallas as pl
from jax.experimental.pallas import tpu as pltpu
from jax.sharding import Mesh, PartitionSpec as P

D = 7168
CAP = 8
ROWS = 128
FEAT = 896
WIDE = 1024
BOTH = WIDE + FEAT
HID = 256
EPSILON = 1e-06
PLACES = ((0, 1, 3, 2), (0, 3, 1, 2))

f32 = jnp.float32
bf16 = jnp.bfloat16
SMEM, VMEM, COPY, HBM = "smem", "vmem", "copy", "hbm"


def nn(a, b):
    return lax.dot_general(a, b, (((1,), (0,)), ((), ())), preferred_element_type=f32)


def nt(a, b):
    return lax.dot_general(a, b, (((1,), (1,)), ((), ())), preferred_element_type=f32)


def tn(a, b):
    return lax.dot_general(a, b, (((0,), (0,)), ((), ())), preferred_element_type=f32)


def local_call(kernel, inputs, outputs, mib, cost, scratch=()):
    in_specs, args = [], []
    for kind, value in inputs:
        space = {SMEM: pltpu.SMEM, HBM: pl.ANY}.get(kind, pltpu.VMEM)
        in_specs.append(pl.BlockSpec(memory_space=space))
        if kind != SMEM:
            value = pltpu.with_memory_space_constraint(value, pltpu.VMEM if kind == VMEM else pltpu.HBM)
        args.append(value)
    out_shape, out_specs = [], []
    for kind, shape, dtype in outputs:
        space = {VMEM: pltpu.VMEM, HBM: pltpu.HBM}.get(kind, jax.ShapeDtypeStruct)
        out_shape.append(space(shape, dtype))
        out_specs.append(pl.BlockSpec(memory_space=pl.ANY if kind == HBM else pltpu.VMEM))
    return pl.pallas_call(
        kernel,
        out_shape=out_shape,
        in_specs=in_specs,
        out_specs=out_specs,
        scratch_shapes=list(scratch),
        compiler_params=pltpu.CompilerParams(vmem_limit_bytes=mib * 2**20),
        cost_estimate=pl.CostEstimate(flops=cost[0], bytes_accessed=cost[1], transcendentals=0),
    )(*args)


def held(*values):
    return [(VMEM, value) for value in values]


def fetched(*values):
    return [(COPY, value) for value in values]


def split_two(value):
    high = value.astype(bf16)
    low = (value - high.astype(f32)).astype(bf16)
    return high, low


def slot_matches(ids, slots):
    live = (ids < 16) & (slots >= 0) & (slots < CAP)
    target = jnp.where(live, ids * CAP + slots, ROWS)
    slot = lax.broadcasted_iota(jnp.int32, (ROWS, ROWS), 0)
    return live, [slot == target[k : k + 1, :] for k in range(8)]


def pick_rows(matches, parent):
    pick = matches[0]
    for match in matches[1:]:
        pick = pick | match
    pick = jnp.where(pick, 1.0, 0.0).astype(bf16)
    row = lax.broadcasted_iota(jnp.int32, (ROWS, ROWS), 0)
    from_parent = jnp.where(row == parent, 1.0, 0.0).astype(bf16)
    return pick, nt(pick, from_parent).astype(bf16)


def mix_of(matches, gates):
    mix = jnp.zeros((ROWS, ROWS), f32)
    for k, match in enumerate(matches):
        mix = mix + jnp.where(match, gates[k : k + 1, :], 0.0)
    return mix


def prepare(hidden, gain, source, ids, slots, gates, cotangent, rows, kept):
    _, matches = slot_matches(ids[...], slots[...])
    pick, select = pick_rows(matches, source[...] & (ROWS - 1))
    gate = jnp.sum(mix_of(matches, gates[...]), axis=1, keepdims=True)
    beam = nn(select, hidden[...])
    rows[:, :FEAT] = (beam * gain[...][None, :]).astype(bf16)
    square = jnp.sum(beam * beam, axis=1, keepdims=True) * (1.0 / D)
    high, low = split_two(square)
    lane = lax.broadcasted_iota(jnp.int32, (ROWS, WIDE - FEAT), 1)
    tail = jnp.where(lane == 0, high.astype(f32), jnp.where(lane == 1, low.astype(f32), 0.0))
    rows[:, FEAT:WIDE] = tail.astype(bf16)
    rows[:, WIDE:] = (nn(pick, cotangent[...]) * gate).astype(bf16)
    kept[...] = hidden[...]


def heads_here():
    y, core = lax.axis_index("y"), lax.axis_index("core")
    heads = []
    for side in (core, 1 - core):
        heads += [(y ^ jnp.where(side == 0, PLACES[0][i], PLACES[1][i])) * 2 + side for i in range(4)]
    return jnp.stack(heads).astype(jnp.int32)


def head_at(heads, place, side):
    return heads[4 * side + place]


def row_part(head):
    return pl.ds(pl.multiple_of(head * FEAT, FEAT), FEAT)


def column_part(head):
    return pl.ds(pl.multiple_of(head * FEAT, 128), FEAT)


def weight_copies(where, side, place, weights, targets, sems):
    head = head_at(where, place, side)
    w_gate, w_up, w_down = weights
    sources = (w_gate.at[0, row_part(head), :], w_up.at[0, row_part(head), :], w_down.at[0, :, column_part(head)])
    copies = [pltpu.make_async_copy(*pair, sems.at[j]) for j, pair in enumerate(zip(sources, targets))]
    for copy in copies:
        copy.start()
    return copies


def add_blocks(copies, blocks, parts, totals, squares):
    gate, up, hid = totals
    for n, block in enumerate(blocks):
        squares = squares + block[:, FEAT:WIDE].astype(f32)
        for copy in copies[n]:
            copy.wait()
        gate = gate + nn(block[:, :FEAT], parts[0][n])
        up = up + nn(block[:, :FEAT], parts[1][n])
        hid = hid + nt(block[:, WIDE:], parts[2][n])
    return (gate, up, hid), squares


def own_blocks(where, own, sibling, w_gate, w_up, w_down, *refs):
    gate, up, hid, mean, late_gate, late_up, late_down, *parts, late, sems = refs
    weights = (w_gate, w_up, w_down)
    copies = [weight_copies(where, side, 0, weights, [p.at[side] for p in parts], sems.at[side]) for side in range(2)]
    last = [
        weight_copies(where, side, 3, weights, (late_gate.at[side], late_up.at[side], late.at[side]), sems.at[2 + side])
        for side in range(2)
    ]
    zero = jnp.zeros((ROWS, HID), f32)
    squares = jnp.zeros((ROWS, WIDE - FEAT), f32)
    totals, squares = add_blocks(copies, (own, sibling), parts, (zero, zero, zero), squares)
    for side in range(2):
        for copy in last[side]:
            copy.wait()
        late_down[side] = late[side].T
    gate[...], up[...], hid[...] = totals
    mean[...] = squares


def first_block(where, own, w_gate, w_up, w_down, *refs):
    sums, results, next_parts, (*parts, sems) = refs[:4], refs[4:8], refs[8:11], refs[11:]
    weights = (w_gate, w_up, w_down)
    copies = [weight_copies(where, 0, 1, weights, [p.at[0] for p in parts], sems.at[0])]
    following = [
        weight_copies(where, side, place, weights, [p.at[n] for p in next_parts], sems.at[1 + n])
        for n, (side, place) in enumerate(((1, 1), (0, 2), (1, 2)))
    ]
    totals, squares = add_blocks(copies, (own,), parts, [ref[...] for ref in sums[:3]], sums[3][...])
    for copies in following:
        for copy in copies:
            copy.wait()
    results[0][...], results[1][...], results[2][...] = totals
    results[3][...] = squares


def next_blocks(first_low, first_high, second, second_low, second_high, *refs):
    sums, parts, results = refs[:4], refs[4:7], refs[7:]
    first_sibling = jnp.concatenate([first_low[...], first_high[...]], axis=0)
    second_sibling = jnp.concatenate([second_low[...], second_high[...]], axis=0)
    blocks = (first_sibling, second, second_sibling)
    totals, squares = add_blocks(((), (), ()), blocks, parts, [ref[...] for ref in sums[:3]], sums[3][...])
    results[0][...], results[1][...], results[2][...] = totals
    results[3][...] = squares


def expert_terms(where, act, d_gate, d_up, w_down, w_gate, w_up, side, results, tail):
    for i in results:
        head = head_at(where, i, side)
        rows, columns = row_part(head), column_part(head)
        results[i][:, :FEAT] = nn(act, w_down[0, :, columns]).astype(bf16)
        term = nt(d_gate, w_gate[0, rows, :]) + nt(d_up, w_up[0, rows, :])
        results[i][:, FEAT : FEAT + FEAT] = term.astype(bf16)
        results[i][:, FEAT + FEAT :] = tail


def last_blocks(where, *refs):
    blocks, (late_gate, late_up, late_down) = refs[:2], refs[2:5]
    first_gate, first_up, first_hid, mean, w_down, w_gate, w_up = refs[5:12]
    act, grad_gate, grad_up, tail_out, *other = refs[12:]
    gate, up, hid = first_gate[...], first_up[...], first_hid[...]
    squares = mean[...]
    for side, block in enumerate(blocks):
        squares = squares + block[:, FEAT:WIDE].astype(f32)
        gate = gate + nn(block[:, :FEAT], late_gate[side])
        up = up + nn(block[:, :FEAT], late_up[side])
        hid = hid + nn(block[:, WIDE:], late_down[side])
    inverse = lax.rsqrt(jnp.sum(squares, axis=1, keepdims=True) + EPSILON)
    gate = gate * inverse
    up = up * inverse
    sigmoid = jax.nn.sigmoid(gate)
    hidden_act = (gate * sigmoid * up).astype(bf16)
    score = jnp.sum(hidden_act.astype(f32) * hid, axis=1, keepdims=True)
    scaled = hid * inverse
    d_gate = (scaled * up * sigmoid * (1.0 + gate * (1.0 - sigmoid))).astype(bf16)
    d_up = (scaled * gate * sigmoid).astype(bf16)
    act[...] = hidden_act
    grad_gate[...] = d_gate
    grad_up[...] = d_up
    dot = jnp.sum(d_gate.astype(f32) * gate + d_up.astype(f32) * up, axis=1, keepdims=True)
    dot = dot * inverse * (1.0 / D)
    lane = lax.broadcasted_iota(jnp.int32, (ROWS, WIDE - FEAT), 1)
    me = 2 * head_at(where, 0, 0)
    tail = jnp.zeros((ROWS, WIDE - FEAT), f32)
    for base, value in ((0, score), (64, dot)):
        high, low = split_two(value)
        tail = jnp.where(lane == base + me, high.astype(f32), tail)
        tail = jnp.where(lane == base + me + 1, low.astype(f32), tail)
    tail = tail.astype(bf16)
    tail_out[...] = tail
    expert_terms(where, hidden_act, d_gate, d_up, w_down, w_gate, w_up, 1, {3: other[3], 2: other[2], 1: other[1], 0: other[0]}, tail)


def own_across(where, act, grad_gate, grad_up, tail, w_down, w_gate, w_up, across):
    expert_terms(where, act[...], grad_gate[...], grad_up[...], w_down, w_gate, w_up, 0, {3: across}, tail[...])


def own_terms(where, act, grad_gate, grad_up, tail, w_down, w_gate, w_up, mine, first, second):
    results = {2: second, 1: first, 0: mine}
    expert_terms(where, act[...], grad_gate[...], grad_up[...], w_down, w_gate, w_up, 0, results, tail[...])


def weight_grads(where, *refs):
    blocks, (act, grad_gate, grad_up, out_gate, out_up, out_down) = refs[:10], refs[10:16]
    held_rows, buf_gate, buf_up, buf_down, load_sems, store_sems = refs[16:]
    loads = [[] for _ in range(8)]
    for i, block in enumerate(blocks):
        n = i if i < 5 else (i + 5) // 2 if i < 9 else 7
        start = ROWS // 2 if i in (6, 8) else 0
        rows = slice(start, start + block.shape[0])
        loads[n].append(pltpu.make_async_copy(block, held_rows.at[n, rows, :], load_sems.at[i]))
        loads[n][-1].start()
    act_t = act[...].T
    stores = []
    for n in range(8):
        for load in loads[n]:
            load.wait()
        head = head_at(where, n % 4, n // 4)
        beam_t = held_rows[n, :, :FEAT].T
        for j, (left, right, buf, target) in enumerate(
            (
                (act_t, held_rows[n, :, WIDE:], buf_down, out_down.at[0, :, column_part(head)]),
                (beam_t, grad_gate[...], buf_gate, out_gate.at[0, row_part(head), :]),
                (beam_t, grad_up[...], buf_up, out_up.at[0, row_part(head), :]),
            )
        ):
            buf[n] = nn(left, right).astype(bf16)
            stores.append(pltpu.make_async_copy(buf.at[n], target, store_sems.at[n, j]))
            stores[-1].start()
    for store in stores:
        store.wait()


def route_tables(ids, slots, gates, source, gain, select, mix, targets, kept_gates, kept_gain):
    live, matches = slot_matches(ids[...], slots[...])
    select[...] = pick_rows(matches, source[...] & (ROWS - 1))[1]
    rest = mix_of(matches, gates[...])
    for i in range(3):
        mix[i] = rest.astype(bf16)
        rest = rest - mix[i].astype(f32)
    targets[...] = jnp.where(live, ids[...] * CAP + slots[...], ROWS)
    kept_gates[...] = gates[...]
    kept_gain[...] = gain[...][None, :]


def finish(home, hidden, select, mix, targets, gates, gain, moe, grad_hidden, grad_gates):
    rows = home[:, :FEAT]
    moe[...] = (tn(mix[0], rows) + (tn(mix[1], rows) + tn(mix[2], rows))).astype(bf16)
    tail = home[:, FEAT + FEAT :].astype(f32)
    lane = lax.broadcasted_iota(jnp.int32, tail.shape, 1)
    score = jnp.sum(jnp.where(lane < 64, tail, 0.0), axis=1, keepdims=True)
    dot = jnp.sum(jnp.where(lane < 64, 0.0, tail), axis=1, keepdims=True)
    slot = lax.broadcasted_iota(jnp.int32, (ROWS, ROWS), 0)
    found = [
        jnp.sum(jnp.where(slot == targets[k : k + 1, :], score, 0.0), axis=0, keepdims=True) for k in range(8)
    ]
    found = jnp.concatenate(found, axis=0)
    grad_gates[...] = jnp.where(targets[...] < ROWS, found / gates[...], 0.0)
    picks = select[...]
    back = tn(picks, home[:, FEAT : FEAT + FEAT]) * gain[...]
    dots = jnp.where(picks.astype(f32) > 0, dot, 0.0)
    per_parent = jnp.sum(dots.T, axis=1, keepdims=True)
    grad_hidden[...] = (back - hidden[...].astype(f32) * per_parent).astype(bf16)


def to_place(values, place):
    pairs = [(2 * y + core, 2 * (y ^ PLACES[core][place]) + core) for y in range(4) for core in range(2)]
    return lax.ppermute(values, ("y", "core"), pairs)


def to_sibling(values):
    return lax.ppermute(values, "core", [(0, 1), (1, 0)])


def sent_home(sums, beside):
    mine, first, second, across = sums
    passing, beside = lax.optimization_barrier((to_place(across, 2), beside))
    first = joined(first, passing)
    return joined(mine, to_place(first, 1), to_place(second, 2)), beside


def joined(*parts):
    total = parts[0].astype(f32)
    for part in parts[1:]:
        total = total + part.astype(f32)
    return total.astype(bf16)


def exchange(rows):
    width = rows.shape[1]
    pieces = rows.reshape(16, CAP, width)
    return lax.all_to_all(pieces, ("x", "z"), 0, 0, tiled=True).reshape(ROWS, width)


def on_device(
    hidden, norm_gain, beam_src, route_ids, route_slots, route_gates, w_gate, w_up, w_down, out_grad
):
    where = (SMEM, heads_here())
    gain = norm_gain
    source = beam_src.reshape(1, ROWS)
    ids, slots, gates = route_ids.T, route_slots.T, route_gates.T
    rows, kept = local_call(
        prepare,
        fetched(hidden, gain, source, ids, slots, gates, out_grad),
        [(VMEM, (ROWS, WIDE + FEAT), bf16), (VMEM, (ROWS, FEAT), bf16)],
        8,
        (0, 1000),
    )
    sent = exchange(rows)
    weights = [(HBM, w_gate), (HBM, w_up), (HBM, w_down)]
    sums = [*[(VMEM, (ROWS, HID), f32)] * 3, (VMEM, (ROWS, WIDE - FEAT), f32)]
    sibling = to_sibling(sent)
    *early, late_gate, late_up, late_down = local_call(
        own_blocks,
        [where, *held(sent, sibling), *weights],
        [*sums, *[(VMEM, (2, FEAT, HID), bf16)] * 3],
        8,
        (0, 1000),
        scratch=(
            pltpu.VMEM((2, FEAT, HID), bf16),
            pltpu.VMEM((2, FEAT, HID), bf16),
            pltpu.VMEM((2, HID, FEAT), bf16),
            pltpu.VMEM((2, HID, FEAT), bf16),
            pltpu.SemaphoreType.DMA((4, 3)),
        ),
    )
    later, *early = lax.optimization_barrier((sent, *early))
    first, second = to_place(sent, 1), to_place(later, 2)
    first, *early = lax.optimization_barrier((first, *early))
    across = to_place(first, 2)
    first_halves = [to_sibling(first[: ROWS // 2]), to_sibling(first[ROWS // 2 :])]
    *early, next_gate, next_up, next_down = local_call(
        first_block,
        [where, *held(first), *weights, *held(*early)],
        [
            *sums,
            (VMEM, (3, FEAT, HID), bf16),
            (VMEM, (3, FEAT, HID), bf16),
            (VMEM, (3, HID, FEAT), bf16),
        ],
        8,
        (0, 1000),
        scratch=(
            pltpu.VMEM((1, FEAT, HID), bf16),
            pltpu.VMEM((1, FEAT, HID), bf16),
            pltpu.VMEM((1, HID, FEAT), bf16),
            pltpu.SemaphoreType.DMA((4, 3)),
        ),
    )
    second, *early = lax.optimization_barrier((second, *early))
    second_halves = [to_sibling(second[: ROWS // 2]), to_sibling(second[ROWS // 2 :])]
    near = [sent, first, second]
    near_sibling = [sibling, *first_halves, *second_halves]
    gate, up, hid, mean = local_call(
        next_blocks,
        held(*first_halves, second, *second_halves, *early, next_gate, next_up, next_down),
        sums,
        4,
        (10**9, 1000),
    )
    across, mean = lax.optimization_barrier((across, mean))
    across_sibling = to_sibling(across)
    act, d_gate, d_up, tail, *other = local_call(
        last_blocks,
        [where, *held(across, across_sibling, late_gate, late_up, late_down, gate, up, hid, mean, w_down, w_gate, w_up)],
        [
            *[(VMEM, (ROWS, HID), bf16)] * 3,
            (VMEM, (ROWS, WIDE - FEAT), bf16),
            *[(VMEM, (ROWS, BOTH), bf16)] * 4,
        ],
        4,
        (10**9, 1000),
    )
    theirs = [to_sibling(value) for value in other]
    term_inputs = [where, *held(act, d_gate, d_up, tail, w_down, w_gate, w_up)]
    (across_term,) = local_call(own_across, term_inputs, [(VMEM, (ROWS, BOTH), bf16)], 4, (0, 1000))
    across_sum, later_tail = lax.optimization_barrier((joined(across_term, theirs[3]), tail))
    term_inputs[4] = (VMEM, later_tail)
    own = local_call(own_terms, term_inputs, [(VMEM, (ROWS, BOTH), bf16)] * 3, 4, (0, 1000))
    blocks = [(HBM, block) for block in (*near, across, *near_sibling, across_sibling)]
    home_sums = [joined(mine, term) for mine, term in zip(own, theirs)] + [across_sum]
    home_sums[3], late_gates = lax.optimization_barrier((home_sums[3], gates))
    tables = local_call(
        route_tables,
        fetched(ids, slots, late_gates, source, gain),
        [
            (VMEM, (ROWS, ROWS), bf16),
            (VMEM, (3, ROWS, ROWS), bf16),
            (VMEM, (8, ROWS), jnp.int32),
            (VMEM, (8, ROWS), f32),
            (VMEM, (1, FEAT), f32),
        ],
        4,
        (0, 1000),
    )
    home_sums, tables = sent_home(home_sums, tables)
    grads = local_call(
        weight_grads,
        [where, *blocks, *fetched(act, d_gate, d_up)],
        [(HBM, (1, D, HID), bf16), (HBM, (1, D, HID), bf16), (HBM, (1, HID, D), bf16)],
        20,
        (2 * 3 * 2 * ROWS * D * HID, 22 * 10**6),
        scratch=(
            pltpu.VMEM((8, ROWS, BOTH), bf16),
            pltpu.VMEM((8, FEAT, HID), bf16),
            pltpu.VMEM((8, FEAT, HID), bf16),
            pltpu.VMEM((8, HID, FEAT), bf16),
            pltpu.SemaphoreType.DMA((10,)),
            pltpu.SemaphoreType.DMA((8, 3)),
        ),
    )
    home_sums, *grads = lax.optimization_barrier((home_sums, *grads))
    home = exchange(home_sums)
    moe, grad_hidden, grad_gates = local_call(
        finish,
        held(home, kept, *tables),
        [(COPY, (ROWS, FEAT), bf16), (COPY, (ROWS, FEAT), bf16), (COPY, (8, ROWS), f32)],
        4,
        (0, 1000),
    )
    return (moe, grad_hidden, grad_gates.T, *grads)


def solution(mesh):
    split = Mesh(mesh.devices.reshape(4, 2, 4, 4), ("y", "core", "x", "z"))
    heads, seq = ("y", "core"), ("x", "z")
    return jax.shard_map(
        on_device,
        mesh=split,
        in_specs=(
            P(seq, heads),
            P(heads),
            P(seq),
            P(seq, None),
            P(seq, None),
            P(seq, None),
            P(seq, None, heads),
            P(seq, None, heads),
            P(seq, heads, None),
            P(seq, heads),
        ),
        out_specs=(
            P(seq, heads),
            P(seq, heads),
            P(seq, None),
            P(seq, None, heads),
            P(seq, None, heads),
            P(seq, heads, None),
        ),
        check_vma=False,
    )
```

```python
import functools

import jax
import jax.numpy as jnp
from jax import lax
from jax.experimental import pallas as pl
from jax.experimental.pallas import tpu as pltpu
from jax.sharding import Mesh, PartitionSpec as P

D = 7168
CAP = 8
ROWS = 128
FEAT = 896
WIDE = 1024
BOTH = WIDE + FEAT
HID = 256
EPSILON = 1e-06
PLACES = ((0, 1, 3, 2), (0, 3, 1, 2))

f32 = jnp.float32
bf16 = jnp.bfloat16
SMEM, VMEM, COPY, HBM = "smem", "vmem", "copy", "hbm"


def nn(a, b):
    return lax.dot_general(a, b, (((1,), (0,)), ((), ())), preferred_element_type=f32)


def nt(a, b):
    return lax.dot_general(a, b, (((1,), (1,)), ((), ())), preferred_element_type=f32)


def tn(a, b):
    return lax.dot_general(a, b, (((0,), (0,)), ((), ())), preferred_element_type=f32)


def local_call(kernel, inputs, outputs, mib, cost, scratch=()):
    in_specs, args = [], []
    for kind, value in inputs:
        space = {SMEM: pltpu.SMEM, HBM: pl.ANY}.get(kind, pltpu.VMEM)
        in_specs.append(pl.BlockSpec(memory_space=space))
        if kind != SMEM:
            value = pltpu.with_memory_space_constraint(value, pltpu.VMEM if kind == VMEM else pltpu.HBM)
        args.append(value)
    out_shape, out_specs = [], []
    for kind, shape, dtype in outputs:
        space = {VMEM: pltpu.VMEM, HBM: pltpu.HBM}.get(kind, jax.ShapeDtypeStruct)
        out_shape.append(space(shape, dtype))
        out_specs.append(pl.BlockSpec(memory_space=pl.ANY if kind == HBM else pltpu.VMEM))
    return pl.pallas_call(
        kernel,
        out_shape=out_shape,
        in_specs=in_specs,
        out_specs=out_specs,
        scratch_shapes=list(scratch),
        compiler_params=pltpu.CompilerParams(vmem_limit_bytes=mib * 2**20),
        cost_estimate=pl.CostEstimate(flops=cost[0], bytes_accessed=cost[1], transcendentals=0),
    )(*args)


def held(*values):
    return [(VMEM, value) for value in values]


def fetched(*values):
    return [(COPY, value) for value in values]


def split_two(value):
    high = value.astype(bf16)
    low = (value - high.astype(f32)).astype(bf16)
    return high, low


def slot_matches(ids, slots):
    live = (ids < 16) & (slots >= 0) & (slots < CAP)
    target = jnp.where(live, ids * CAP + slots, ROWS)
    slot = lax.broadcasted_iota(jnp.int32, (ROWS, ROWS), 0)
    return live, [slot == target[k : k + 1, :] for k in range(8)]


def pick_rows(matches, parent):
    pick = matches[0]
    for match in matches[1:]:
        pick = pick | match
    pick = jnp.where(pick, 1.0, 0.0).astype(bf16)
    row = lax.broadcasted_iota(jnp.int32, (ROWS, ROWS), 0)
    from_parent = jnp.where(row == parent, 1.0, 0.0).astype(bf16)
    return pick, nt(pick, from_parent).astype(bf16)


def mix_of(matches, gates):
    mix = jnp.zeros((ROWS, ROWS), f32)
    for k, match in enumerate(matches):
        mix = mix + jnp.where(match, gates[k : k + 1, :], 0.0)
    return mix


def prepare(hidden, gain, source, ids, slots, gates, cotangent, rows, kept):
    _, matches = slot_matches(ids[...], slots[...])
    pick, select = pick_rows(matches, source[...] & (ROWS - 1))
    gate = jnp.sum(mix_of(matches, gates[...]), axis=1, keepdims=True)
    beam = nn(select, hidden[...])
    rows[:, :FEAT] = (beam * gain[...][None, :]).astype(bf16)
    square = jnp.sum(beam * beam, axis=1, keepdims=True) * (1.0 / D)
    high, low = split_two(square)
    lane = lax.broadcasted_iota(jnp.int32, (ROWS, WIDE - FEAT), 1)
    tail = jnp.where(lane == 0, high.astype(f32), jnp.where(lane == 1, low.astype(f32), 0.0))
    rows[:, FEAT:WIDE] = tail.astype(bf16)
    rows[:, WIDE:] = (nn(pick, cotangent[...]) * gate).astype(bf16)
    kept[...] = hidden[...]


def heads_here():
    y, core = lax.axis_index("y"), lax.axis_index("core")
    heads = []
    for side in (core, 1 - core):
        heads += [(y ^ jnp.where(side == 0, PLACES[0][i], PLACES[1][i])) * 2 + side for i in range(4)]
    return jnp.stack(heads).astype(jnp.int32)


def head_at(heads, place, side):
    return heads[4 * side + place]


def row_part(head):
    return pl.ds(pl.multiple_of(head * FEAT, FEAT), FEAT)


def column_part(head):
    return pl.ds(pl.multiple_of(head * FEAT, 128), FEAT)


def weight_copies(where, side, place, weights, targets, sems):
    head = head_at(where, place, side)
    w_gate, w_up, w_down = weights
    sources = (w_gate.at[0, row_part(head), :], w_up.at[0, row_part(head), :], w_down.at[0, :, column_part(head)])
    copies = [pltpu.make_async_copy(*pair, sems.at[j]) for j, pair in enumerate(zip(sources, targets))]
    for copy in copies:
        copy.start()
    return copies


def add_blocks(copies, blocks, parts, totals, squares):
    gate, up, hid = totals
    for n, block in enumerate(blocks):
        squares = squares + block[:, FEAT:WIDE].astype(f32)
        for copy in copies[n]:
            copy.wait()
        gate = gate + nn(block[:, :FEAT], parts[0][n])
        up = up + nn(block[:, :FEAT], parts[1][n])
        hid = hid + nt(block[:, WIDE:], parts[2][n])
    return (gate, up, hid), squares


def own_blocks(where, own, sibling, w_gate, w_up, w_down, *refs):
    gate, up, hid, mean, *parts, sems = refs
    weights = (w_gate, w_up, w_down)
    copies = [weight_copies(where, side, 0, weights, [p.at[side] for p in parts], sems.at[side]) for side in range(2)]
    zero = jnp.zeros((ROWS, HID), f32)
    squares = jnp.zeros((ROWS, WIDE - FEAT), f32)
    totals, squares = add_blocks(copies, (own, sibling), parts, (zero, zero, zero), squares)
    gate[...], up[...], hid[...] = totals
    mean[...] = squares


def first_block(where, own, w_gate, w_up, w_down, *refs):
    sums, results, (*parts, sems) = refs[:4], refs[4:8], refs[8:]
    copies = [weight_copies(where, 0, 1, (w_gate, w_up, w_down), [p.at[0] for p in parts], sems)]
    totals, squares = add_blocks(copies, (own,), parts, [ref[...] for ref in sums[:3]], sums[3][...])
    results[0][...], results[1][...], results[2][...] = totals
    results[3][...] = squares


def next_blocks(where, first_low, first_high, second, second_low, second_high, *refs):
    sums, (w_gate, w_up, w_down), results = refs[:4], refs[4:7], refs[7:]
    first_sibling = jnp.concatenate([first_low[...], first_high[...]], axis=0)
    second_sibling = jnp.concatenate([second_low[...], second_high[...]], axis=0)
    totals, squares = [ref[...] for ref in sums[:3]], sums[3][...]
    for place, side, block in ((1, 1, first_sibling), (2, 0, second), (2, 1, second_sibling)):
        head = head_at(where, place, side)
        rows, columns = row_part(head), column_part(head)
        parts = ([w_gate[0, rows, :]], [w_up[0, rows, :]], [w_down[0, :, columns]])
        totals, squares = add_blocks(((),), (block,), parts, totals, squares)
    results[0][...], results[1][...], results[2][...] = totals
    results[3][...] = squares


def expert_terms(where, act, d_gate, d_up, w_down, w_gate, w_up, side, results, tail):
    for i in results:
        head = head_at(where, i, side)
        rows, columns = row_part(head), column_part(head)
        results[i][:, :FEAT] = nn(act, w_down[0, :, columns]).astype(bf16)
        term = nt(d_gate, w_gate[0, rows, :]) + nt(d_up, w_up[0, rows, :])
        results[i][:, FEAT : FEAT + FEAT] = term.astype(bf16)
        results[i][:, FEAT + FEAT :] = tail


def last_blocks(where, *refs):
    blocks, (first_gate, first_up, first_hid, mean), (w_down, w_gate, w_up) = refs[:2], refs[2:6], refs[6:9]
    act, grad_gate, grad_up, tail_out, across_other = refs[9:]
    gate, up, hid = first_gate[...], first_up[...], first_hid[...]
    squares = mean[...]
    for side, block in enumerate(blocks):
        squares = squares + block[:, FEAT:WIDE].astype(f32)
        head = head_at(where, 3, side)
        rows, columns = row_part(head), column_part(head)
        gate = gate + nn(block[:, :FEAT], w_gate[0, rows, :])
        up = up + nn(block[:, :FEAT], w_up[0, rows, :])
        hid = hid + nt(block[:, WIDE:], w_down[0, :, columns])
    inverse = lax.rsqrt(jnp.sum(squares, axis=1, keepdims=True) + EPSILON)
    gate = gate * inverse
    up = up * inverse
    sigmoid = jax.nn.sigmoid(gate)
    hidden_act = (gate * sigmoid * up).astype(bf16)
    score = jnp.sum(hidden_act.astype(f32) * hid, axis=1, keepdims=True)
    scaled = hid * inverse
    d_gate = (scaled * up * sigmoid * (1.0 + gate * (1.0 - sigmoid))).astype(bf16)
    d_up = (scaled * gate * sigmoid).astype(bf16)
    act[...] = hidden_act
    grad_gate[...] = d_gate
    grad_up[...] = d_up
    dot = jnp.sum(d_gate.astype(f32) * gate + d_up.astype(f32) * up, axis=1, keepdims=True)
    dot = dot * inverse * (1.0 / D)
    lane = lax.broadcasted_iota(jnp.int32, (ROWS, WIDE - FEAT), 1)
    me = 2 * head_at(where, 0, 0)
    tail = jnp.zeros((ROWS, WIDE - FEAT), f32)
    for base, value in ((0, score), (64, dot)):
        high, low = split_two(value)
        tail = jnp.where(lane == base + me, high.astype(f32), tail)
        tail = jnp.where(lane == base + me + 1, low.astype(f32), tail)
    tail = tail.astype(bf16)
    tail_out[...] = tail
    expert_terms(where, hidden_act, d_gate, d_up, w_down, w_gate, w_up, 1, {3: across_other}, tail)


def own_across(where, act, grad_gate, grad_up, tail, w_down, w_gate, w_up, across, second_other):
    terms = (where, act[...], grad_gate[...], grad_up[...], w_down, w_gate, w_up)
    expert_terms(*terms, 0, {3: across}, tail[...])
    expert_terms(*terms, 1, {2: second_other}, tail[...])


def near_terms(side, where, act, grad_gate, grad_up, tail, w_down, w_gate, w_up, *terms):
    results = {i: terms[i] for i in reversed(range(len(terms)))}
    expert_terms(where, act[...], grad_gate[...], grad_up[...], w_down, w_gate, w_up, side, results, tail[...])


def weight_grads(where, *refs):
    blocks, (act, grad_gate, grad_up, out_gate, out_up, out_down) = refs[:10], refs[10:16]
    held_rows, buf_gate, buf_up, buf_down, load_sems, store_sems = refs[16:]
    loads = [[] for _ in range(8)]
    for i, block in enumerate(blocks):
        n = i if i < 5 else (i + 5) // 2 if i < 9 else 7
        start = ROWS // 2 if i in (6, 8) else 0
        rows = slice(start, start + block.shape[0])
        loads[n].append(pltpu.make_async_copy(block, held_rows.at[n, rows, :], load_sems.at[i]))
        loads[n][-1].start()
    act_t = act[...].T
    stores = []
    for n in range(8):
        for load in loads[n]:
            load.wait()
        head = head_at(where, n % 4, n // 4)
        beam_t = held_rows[n, :, :FEAT].T
        for j, (left, right, buf, target) in enumerate(
            (
                (act_t, held_rows[n, :, WIDE:], buf_down, out_down.at[0, :, column_part(head)]),
                (beam_t, grad_gate[...], buf_gate, out_gate.at[0, row_part(head), :]),
                (beam_t, grad_up[...], buf_up, out_up.at[0, row_part(head), :]),
            )
        ):
            buf[n] = nn(left, right).astype(bf16)
            stores.append(pltpu.make_async_copy(buf.at[n], target, store_sems.at[n, j]))
            stores[-1].start()
    for store in stores:
        store.wait()


def route_tables(ids, slots, gates, source, gain, select, mix, targets, kept_gates, kept_gain):
    live, matches = slot_matches(ids[...], slots[...])
    select[...] = pick_rows(matches, source[...] & (ROWS - 1))[1]
    rest = mix_of(matches, gates[...])
    for i in range(3):
        mix[i] = rest.astype(bf16)
        rest = rest - mix[i].astype(f32)
    targets[...] = jnp.where(live, ids[...] * CAP + slots[...], ROWS)
    kept_gates[...] = gates[...]
    kept_gain[...] = gain[...][None, :]


def finish(home, hidden, select, mix, targets, gates, gain, moe, grad_hidden, grad_gates):
    rows = home[:, :FEAT]
    moe[...] = (tn(mix[0], rows) + (tn(mix[1], rows) + tn(mix[2], rows))).astype(bf16)
    tail = home[:, FEAT + FEAT :].astype(f32)
    lane = lax.broadcasted_iota(jnp.int32, tail.shape, 1)
    score = jnp.sum(jnp.where(lane < 64, tail, 0.0), axis=1, keepdims=True)
    dot = jnp.sum(jnp.where(lane < 64, 0.0, tail), axis=1, keepdims=True)
    slot = lax.broadcasted_iota(jnp.int32, (ROWS, ROWS), 0)
    found = [
        jnp.sum(jnp.where(slot == targets[k : k + 1, :], score, 0.0), axis=0, keepdims=True) for k in range(8)
    ]
    found = jnp.concatenate(found, axis=0)
    grad_gates[...] = jnp.where(targets[...] < ROWS, found / gates[...], 0.0)
    picks = select[...]
    back = tn(picks, home[:, FEAT : FEAT + FEAT]) * gain[...]
    dots = jnp.where(picks.astype(f32) > 0, dot, 0.0)
    per_parent = jnp.sum(dots.T, axis=1, keepdims=True)
    grad_hidden[...] = (back - hidden[...].astype(f32) * per_parent).astype(bf16)


def to_place(values, place):
    pairs = [(2 * y + core, 2 * (y ^ PLACES[core][place]) + core) for y in range(4) for core in range(2)]
    return lax.ppermute(values, ("y", "core"), pairs)


def to_sibling(values):
    return lax.ppermute(values, "core", [(0, 1), (1, 0)])


def sent_home(sums, beside):
    mine, first, second, across = sums
    passing, beside = lax.optimization_barrier((to_place(across, 2), beside))
    first = joined(first, passing)
    return joined(mine, to_place(first, 1), to_place(second, 2)), beside


def joined(*parts):
    total = parts[0].astype(f32)
    for part in parts[1:]:
        total = total + part.astype(f32)
    return total.astype(bf16)


def exchange(rows):
    width = rows.shape[1]
    pieces = rows.reshape(16, CAP, width)
    return lax.all_to_all(pieces, ("x", "z"), 0, 0, tiled=True).reshape(ROWS, width)


def on_device(
    hidden, norm_gain, beam_src, route_ids, route_slots, route_gates, w_gate, w_up, w_down, out_grad
):
    where = (SMEM, heads_here())
    gain = norm_gain
    source = beam_src.reshape(1, ROWS)
    ids, slots, gates = route_ids.T, route_slots.T, route_gates.T
    rows, kept = local_call(
        prepare,
        fetched(hidden, gain, source, ids, slots, gates, out_grad),
        [(VMEM, (ROWS, WIDE + FEAT), bf16), (VMEM, (ROWS, FEAT), bf16)],
        8,
        (0, 1000),
    )
    sent = exchange(rows)
    weights = [(HBM, w_gate), (HBM, w_up), (HBM, w_down)]
    sums = [*[(VMEM, (ROWS, HID), f32)] * 3, (VMEM, (ROWS, WIDE - FEAT), f32)]
    sibling = to_sibling(sent)
    early = local_call(
        own_blocks,
        [where, *held(sent, sibling), *weights],
        sums,
        8,
        (0, 1000),
        scratch=(
            pltpu.VMEM((2, FEAT, HID), bf16),
            pltpu.VMEM((2, FEAT, HID), bf16),
            pltpu.VMEM((2, HID, FEAT), bf16),
            pltpu.SemaphoreType.DMA((2, 3)),
        ),
    )
    later, *early = lax.optimization_barrier((sent, *early))
    first, second = to_place(sent, 1), to_place(later, 2)
    first, *early = lax.optimization_barrier((first, *early))
    across = to_place(first, 2)
    first_halves = [to_sibling(first[: ROWS // 2]), to_sibling(first[ROWS // 2 :])]
    early = local_call(
        first_block,
        [where, *held(first), *weights, *held(*early)],
        sums,
        8,
        (0, 1000),
        scratch=(
            pltpu.VMEM((1, FEAT, HID), bf16),
            pltpu.VMEM((1, FEAT, HID), bf16),
            pltpu.VMEM((1, HID, FEAT), bf16),
            pltpu.SemaphoreType.DMA((3,)),
        ),
    )
    second, *early = lax.optimization_barrier((second, *early))
    second_halves = [to_sibling(second[: ROWS // 2]), to_sibling(second[ROWS // 2 :])]
    near = [sent, first, second]
    near_sibling = [sibling, *first_halves, *second_halves]
    gate, up, hid, mean = local_call(
        next_blocks,
        [where, *held(*first_halves, second, *second_halves, *early, w_gate, w_up, w_down)],
        sums,
        4,
        (10**9, 1000),
    )
    across, mean = lax.optimization_barrier((across, mean))
    across_sibling = to_sibling(across)
    act, d_gate, d_up, tail, across_other = local_call(
        last_blocks,
        [where, *held(across, across_sibling, gate, up, hid, mean, w_down, w_gate, w_up)],
        [
            *[(VMEM, (ROWS, HID), bf16)] * 3,
            (VMEM, (ROWS, WIDE - FEAT), bf16),
            (VMEM, (ROWS, BOTH), bf16),
        ],
        4,
        (10**9, 1000),
    )
    term_inputs = [where, *held(act, d_gate, d_up, tail, w_down, w_gate, w_up)]
    across_own, second_other = local_call(own_across, term_inputs, [(VMEM, (ROWS, BOTH), bf16)] * 2, 4, (0, 1000))
    across_sum, later_tail = lax.optimization_barrier((joined(across_own, to_sibling(across_other)), tail))
    term_inputs[4] = (VMEM, later_tail)
    other, own = [
        local_call(functools.partial(near_terms, side), term_inputs, [(VMEM, (ROWS, BOTH), bf16)] * n, 4, (0, 1000))
        for side, n in ((1, 2), (0, 3))
    ]
    theirs = [to_sibling(value) for value in (*other, second_other)]
    blocks = [(HBM, block) for block in (*near, across, *near_sibling, across_sibling)]
    home_sums = [joined(mine, term) for mine, term in zip(own, theirs)] + [across_sum]
    home_sums[3], late_gates = lax.optimization_barrier((home_sums[3], gates))
    tables = local_call(
        route_tables,
        fetched(ids, slots, late_gates, source, gain),
        [
            (VMEM, (ROWS, ROWS), bf16),
            (VMEM, (3, ROWS, ROWS), bf16),
            (VMEM, (8, ROWS), jnp.int32),
            (VMEM, (8, ROWS), f32),
            (VMEM, (1, FEAT), f32),
        ],
        4,
        (0, 1000),
    )
    home_sums, tables = sent_home(home_sums, tables)
    grads = local_call(
        weight_grads,
        [where, *blocks, *fetched(act, d_gate, d_up)],
        [(HBM, (1, D, HID), bf16), (HBM, (1, D, HID), bf16), (HBM, (1, HID, D), bf16)],
        20,
        (2 * 3 * 2 * ROWS * D * HID, 22 * 10**6),
        scratch=(
            pltpu.VMEM((8, ROWS, BOTH), bf16),
            pltpu.VMEM((8, FEAT, HID), bf16),
            pltpu.VMEM((8, FEAT, HID), bf16),
            pltpu.VMEM((8, HID, FEAT), bf16),
            pltpu.SemaphoreType.DMA((10,)),
            pltpu.SemaphoreType.DMA((8, 3)),
        ),
    )
    home_sums, *grads = lax.optimization_barrier((home_sums, *grads))
    home = exchange(home_sums)
    moe, grad_hidden, grad_gates = local_call(
        finish,
        held(home, kept, *tables),
        [(COPY, (ROWS, FEAT), bf16), (COPY, (ROWS, FEAT), bf16), (COPY, (8, ROWS), f32)],
        4,
        (0, 1000),
    )
    return (moe, grad_hidden, grad_gates.T, *grads)


def solution(mesh):
    split = Mesh(mesh.devices.reshape(4, 2, 4, 4), ("y", "core", "x", "z"))
    heads, seq = ("y", "core"), ("x", "z")
    return jax.shard_map(
        on_device,
        mesh=split,
        in_specs=(
            P(seq, heads),
            P(heads),
            P(seq),
            P(seq, None),
            P(seq, None),
            P(seq, None),
            P(seq, None, heads),
            P(seq, None, heads),
            P(seq, heads, None),
            P(seq, heads),
        ),
        out_specs=(
            P(seq, heads),
            P(seq, heads),
            P(seq, None),
            P(seq, None, heads),
            P(seq, None, heads),
            P(seq, heads, None),
        ),
        check_vma=False,
    )
```

```python
import functools

import jax
import jax.numpy as jnp
from jax import lax
from jax.experimental import pallas as pl
from jax.experimental.pallas import tpu as pltpu
from jax.sharding import Mesh, PartitionSpec as P

D = 7168
CAP = 8
ROWS = 128
FEAT = 896
WIDE = 1024
BOTH = WIDE + FEAT
HID = 256
EPSILON = 1e-06
PLACES = ((0, 1, 3, 2), (0, 3, 1, 2))

f32 = jnp.float32
bf16 = jnp.bfloat16
SMEM, VMEM, COPY, HBM = "smem", "vmem", "copy", "hbm"


def nn(a, b):
    return lax.dot_general(a, b, (((1,), (0,)), ((), ())), preferred_element_type=f32)


def nt(a, b):
    return lax.dot_general(a, b, (((1,), (1,)), ((), ())), preferred_element_type=f32)


def tn(a, b):
    return lax.dot_general(a, b, (((0,), (0,)), ((), ())), preferred_element_type=f32)


def local_call(kernel, inputs, outputs, mib, cost, scratch=()):
    in_specs, args = [], []
    for kind, value in inputs:
        space = {SMEM: pltpu.SMEM, HBM: pl.ANY}.get(kind, pltpu.VMEM)
        in_specs.append(pl.BlockSpec(memory_space=space))
        if kind != SMEM:
            value = pltpu.with_memory_space_constraint(value, pltpu.VMEM if kind == VMEM else pltpu.HBM)
        args.append(value)
    out_shape, out_specs = [], []
    for kind, shape, dtype in outputs:
        space = {VMEM: pltpu.VMEM, HBM: pltpu.HBM}.get(kind, jax.ShapeDtypeStruct)
        out_shape.append(space(shape, dtype))
        out_specs.append(pl.BlockSpec(memory_space=pl.ANY if kind == HBM else pltpu.VMEM))
    return pl.pallas_call(
        kernel,
        out_shape=out_shape,
        in_specs=in_specs,
        out_specs=out_specs,
        scratch_shapes=list(scratch),
        compiler_params=pltpu.CompilerParams(vmem_limit_bytes=mib * 2**20),
        cost_estimate=pl.CostEstimate(flops=cost[0], bytes_accessed=cost[1], transcendentals=0),
    )(*args)


def held(*values):
    return [(VMEM, value) for value in values]


def fetched(*values):
    return [(COPY, value) for value in values]


def split_two(value):
    high = value.astype(bf16)
    low = (value - high.astype(f32)).astype(bf16)
    return high, low


def slot_matches(ids, slots):
    live = (ids < 16) & (slots >= 0) & (slots < CAP)
    target = jnp.where(live, ids * CAP + slots, ROWS)
    slot = lax.broadcasted_iota(jnp.int32, (ROWS, ROWS), 0)
    return live, [slot == target[k : k + 1, :] for k in range(8)]


def pick_rows(matches, parent):
    pick = matches[0]
    for match in matches[1:]:
        pick = pick | match
    pick = jnp.where(pick, 1.0, 0.0).astype(bf16)
    row = lax.broadcasted_iota(jnp.int32, (ROWS, ROWS), 0)
    from_parent = jnp.where(row == parent, 1.0, 0.0).astype(bf16)
    return pick, nt(pick, from_parent).astype(bf16)


def mix_of(matches, gates):
    mix = jnp.zeros((ROWS, ROWS), f32)
    for k, match in enumerate(matches):
        mix = mix + jnp.where(match, gates[k : k + 1, :], 0.0)
    return mix


def prepare(hidden, gain, source, ids, slots, gates, cotangent, rows, kept, held_cotangent, sems):
    loads = [
        pltpu.make_async_copy(hidden, kept, sems.at[0]),
        pltpu.make_async_copy(cotangent, held_cotangent, sems.at[1]),
    ]
    for load in loads:
        load.start()
    _, matches = slot_matches(ids[...], slots[...])
    pick, select = pick_rows(matches, source[...] & (ROWS - 1))
    gate = jnp.sum(mix_of(matches, gates[...]), axis=1, keepdims=True)
    loads[0].wait()
    beam = nn(select, kept[...])
    rows[:, :FEAT] = (beam * gain[...][None, :]).astype(bf16)
    square = jnp.sum(beam * beam, axis=1, keepdims=True) * (1.0 / D)
    high, low = split_two(square)
    lane = lax.broadcasted_iota(jnp.int32, (ROWS, WIDE - FEAT), 1)
    tail = jnp.where(lane == 0, high.astype(f32), jnp.where(lane == 1, low.astype(f32), 0.0))
    rows[:, FEAT:WIDE] = tail.astype(bf16)
    loads[1].wait()
    rows[:, WIDE:] = (nn(pick, held_cotangent[...]) * gate).astype(bf16)


def heads_here():
    y, core = lax.axis_index("y"), lax.axis_index("core")
    heads = []
    for side in (core, 1 - core):
        heads += [(y ^ jnp.where(side == 0, PLACES[0][i], PLACES[1][i])) * 2 + side for i in range(4)]
    return jnp.stack(heads).astype(jnp.int32)


def head_at(heads, place, side):
    return heads[4 * side + place]


def row_part(head):
    return pl.ds(pl.multiple_of(head * FEAT, FEAT), FEAT)


def column_part(head):
    return pl.ds(pl.multiple_of(head * FEAT, 128), FEAT)


def weight_copies(where, side, place, weights, targets, sems):
    head = head_at(where, place, side)
    w_gate, w_up, w_down = weights
    sources = (w_gate.at[0, row_part(head), :], w_up.at[0, row_part(head), :], w_down.at[0, :, column_part(head)])
    copies = [pltpu.make_async_copy(*pair, sems.at[j]) for j, pair in enumerate(zip(sources, targets))]
    for copy in copies:
        copy.start()
    return copies


def add_blocks(copies, blocks, parts, totals, squares):
    gate, up, hid = totals
    for n, block in enumerate(blocks):
        squares = squares + block[:, FEAT:WIDE].astype(f32)
        for copy in copies[n]:
            copy.wait()
        gate = gate + nn(block[:, :FEAT], parts[0][n])
        up = up + nn(block[:, :FEAT], parts[1][n])
        hid = hid + nt(block[:, WIDE:], parts[2][n])
    return (gate, up, hid), squares


def own_blocks(where, own, sibling, w_gate, w_up, w_down, *refs):
    gate, up, hid, mean, *parts, sems = refs
    weights = (w_gate, w_up, w_down)
    copies = [weight_copies(where, side, 0, weights, [p.at[side] for p in parts], sems.at[side]) for side in range(2)]
    zero = jnp.zeros((ROWS, HID), f32)
    squares = jnp.zeros((ROWS, WIDE - FEAT), f32)
    totals, squares = add_blocks(copies, (own, sibling), parts, (zero, zero, zero), squares)
    gate[...], up[...], hid[...] = totals
    mean[...] = squares


def first_block(where, own, w_gate, w_up, w_down, *refs):
    sums, results, (*parts, sems) = refs[:4], refs[4:8], refs[8:]
    copies = [weight_copies(where, 0, 1, (w_gate, w_up, w_down), [p.at[0] for p in parts], sems)]
    totals, squares = add_blocks(copies, (own,), parts, [ref[...] for ref in sums[:3]], sums[3][...])
    results[0][...], results[1][...], results[2][...] = totals
    results[3][...] = squares


def next_blocks(where, first_low, first_high, second, second_low, second_high, *refs):
    sums, (w_gate, w_up, w_down), results = refs[:4], refs[4:7], refs[7:]
    first_sibling = jnp.concatenate([first_low[...], first_high[...]], axis=0)
    second_sibling = jnp.concatenate([second_low[...], second_high[...]], axis=0)
    totals, squares = [ref[...] for ref in sums[:3]], sums[3][...]
    for place, side, block in ((1, 1, first_sibling), (2, 0, second), (2, 1, second_sibling)):
        head = head_at(where, place, side)
        rows, columns = row_part(head), column_part(head)
        parts = ([w_gate[0, rows, :]], [w_up[0, rows, :]], [w_down[0, :, columns]])
        totals, squares = add_blocks(((),), (block,), parts, totals, squares)
    results[0][...], results[1][...], results[2][...] = totals
    results[3][...] = squares


def expert_terms(where, act, d_gate, d_up, w_down, w_gate, w_up, side, results, tail):
    for i in results:
        head = head_at(where, i, side)
        rows, columns = row_part(head), column_part(head)
        results[i][:, :FEAT] = nn(act, w_down[0, :, columns]).astype(bf16)
        term = nt(d_gate, w_gate[0, rows, :]) + nt(d_up, w_up[0, rows, :])
        results[i][:, FEAT : FEAT + FEAT] = term.astype(bf16)
        results[i][:, FEAT + FEAT :] = tail


def last_blocks(where, *refs):
    blocks, (first_gate, first_up, first_hid, mean), (w_down, w_gate, w_up) = refs[:2], refs[2:6], refs[6:9]
    act, grad_gate, grad_up, tail_out, across_other = refs[9:]
    gate, up, hid = first_gate[...], first_up[...], first_hid[...]
    squares = mean[...]
    for side, block in enumerate(blocks):
        squares = squares + block[:, FEAT:WIDE].astype(f32)
        head = head_at(where, 3, side)
        rows, columns = row_part(head), column_part(head)
        gate = gate + nn(block[:, :FEAT], w_gate[0, rows, :])
        up = up + nn(block[:, :FEAT], w_up[0, rows, :])
        hid = hid + nt(block[:, WIDE:], w_down[0, :, columns])
    inverse = lax.rsqrt(jnp.sum(squares, axis=1, keepdims=True) + EPSILON)
    gate = gate * inverse
    up = up * inverse
    sigmoid = jax.nn.sigmoid(gate)
    hidden_act = (gate * sigmoid * up).astype(bf16)
    score = jnp.sum(hidden_act.astype(f32) * hid, axis=1, keepdims=True)
    scaled = hid * inverse
    d_gate = (scaled * up * sigmoid * (1.0 + gate * (1.0 - sigmoid))).astype(bf16)
    d_up = (scaled * gate * sigmoid).astype(bf16)
    act[...] = hidden_act
    grad_gate[...] = d_gate
    grad_up[...] = d_up
    dot = jnp.sum(d_gate.astype(f32) * gate + d_up.astype(f32) * up, axis=1, keepdims=True)
    dot = dot * inverse * (1.0 / D)
    lane = lax.broadcasted_iota(jnp.int32, (ROWS, WIDE - FEAT), 1)
    me = 2 * head_at(where, 0, 0)
    tail = jnp.zeros((ROWS, WIDE - FEAT), f32)
    for base, value in ((0, score), (64, dot)):
        high, low = split_two(value)
        tail = jnp.where(lane == base + me, high.astype(f32), tail)
        tail = jnp.where(lane == base + me + 1, low.astype(f32), tail)
    tail = tail.astype(bf16)
    tail_out[...] = tail
    expert_terms(where, hidden_act, d_gate, d_up, w_down, w_gate, w_up, 1, {3: across_other}, tail)


def own_across(where, act, grad_gate, grad_up, tail, w_down, w_gate, w_up, across, second_other):
    terms = (where, act[...], grad_gate[...], grad_up[...], w_down, w_gate, w_up)
    expert_terms(*terms, 0, {3: across}, tail[...])
    expert_terms(*terms, 1, {2: second_other}, tail[...])


def near_terms(side, where, act, grad_gate, grad_up, tail, w_down, w_gate, w_up, *terms):
    results = {i: terms[i] for i in reversed(range(len(terms)))}
    expert_terms(where, act[...], grad_gate[...], grad_up[...], w_down, w_gate, w_up, side, results, tail[...])


def weight_grads(where, *refs):
    blocks, (act, grad_gate, grad_up, out_gate, out_up, out_down) = refs[:10], refs[10:16]
    held_rows, buf_gate, buf_up, buf_down, load_sems, store_sems = refs[16:]
    loads = [[] for _ in range(8)]
    for i, block in enumerate(blocks):
        n = i if i < 5 else (i + 5) // 2 if i < 9 else 7
        start = ROWS // 2 if i in (6, 8) else 0
        rows = slice(start, start + block.shape[0])
        loads[n].append(pltpu.make_async_copy(block, held_rows.at[n, rows, :], load_sems.at[i]))
        loads[n][-1].start()
    act_t = act[...].T
    stores = []
    for n in range(8):
        for load in loads[n]:
            load.wait()
        head = head_at(where, n % 4, n // 4)
        beam_t = held_rows[n, :, :FEAT].T
        for j, (left, right, buf, target) in enumerate(
            (
                (act_t, held_rows[n, :, WIDE:], buf_down, out_down.at[0, :, column_part(head)]),
                (beam_t, grad_gate[...], buf_gate, out_gate.at[0, row_part(head), :]),
                (beam_t, grad_up[...], buf_up, out_up.at[0, row_part(head), :]),
            )
        ):
            buf[n] = nn(left, right).astype(bf16)
            stores.append(pltpu.make_async_copy(buf.at[n], target, store_sems.at[n, j]))
            stores[-1].start()
    for store in stores:
        store.wait()


def route_tables(ids, slots, gates, source, gain, select, mix, targets, kept_gates, kept_gain):
    live, matches = slot_matches(ids[...], slots[...])
    select[...] = pick_rows(matches, source[...] & (ROWS - 1))[1]
    rest = mix_of(matches, gates[...])
    for i in range(3):
        mix[i] = rest.astype(bf16)
        rest = rest - mix[i].astype(f32)
    targets[...] = jnp.where(live, ids[...] * CAP + slots[...], ROWS)
    kept_gates[...] = gates[...]
    kept_gain[...] = gain[...][None, :]


def finish(home, hidden, select, mix, targets, gates, gain, moe, grad_hidden, grad_gates):
    rows = home[:, :FEAT]
    moe[...] = (tn(mix[0], rows) + (tn(mix[1], rows) + tn(mix[2], rows))).astype(bf16)
    tail = home[:, FEAT + FEAT :].astype(f32)
    lane = lax.broadcasted_iota(jnp.int32, tail.shape, 1)
    score = jnp.sum(jnp.where(lane < 64, tail, 0.0), axis=1, keepdims=True)
    dot = jnp.sum(jnp.where(lane < 64, 0.0, tail), axis=1, keepdims=True)
    slot = lax.broadcasted_iota(jnp.int32, (ROWS, ROWS), 0)
    found = [
        jnp.sum(jnp.where(slot == targets[k : k + 1, :], score, 0.0), axis=0, keepdims=True) for k in range(8)
    ]
    found = jnp.concatenate(found, axis=0)
    grad_gates[...] = jnp.where(targets[...] < ROWS, found / gates[...], 0.0)
    picks = select[...]
    back = tn(picks, home[:, FEAT : FEAT + FEAT]) * gain[...]
    dots = jnp.where(picks.astype(f32) > 0, dot, 0.0)
    per_parent = jnp.sum(dots.T, axis=1, keepdims=True)
    grad_hidden[...] = (back - hidden[...].astype(f32) * per_parent).astype(bf16)


def to_place(values, place):
    pairs = [(2 * y + core, 2 * (y ^ PLACES[core][place]) + core) for y in range(4) for core in range(2)]
    return lax.ppermute(values, ("y", "core"), pairs)


def to_sibling(values):
    return lax.ppermute(values, "core", [(0, 1), (1, 0)])


def sent_home(sums, later):
    mine, first, second, across = sums
    first, later = lax.optimization_barrier((joined(first, to_place(across, 2)), later))
    return joined(mine, to_place(first, 1), to_place(second, 2)), later


def joined(*parts):
    total = parts[0].astype(f32)
    for part in parts[1:]:
        total = total + part.astype(f32)
    return total.astype(bf16)


def exchange(rows):
    width = rows.shape[1]
    pieces = rows.reshape(16, CAP, width)
    return lax.all_to_all(pieces, ("x", "z"), 0, 0, tiled=True).reshape(ROWS, width)


def on_device(
    hidden, norm_gain, beam_src, route_ids, route_slots, route_gates, w_gate, w_up, w_down, out_grad
):
    where = (SMEM, heads_here())
    gain = norm_gain
    source = beam_src.reshape(1, ROWS)
    ids, slots, gates = route_ids.T, route_slots.T, route_gates.T
    rows, kept = local_call(
        prepare,
        [(HBM, hidden), *fetched(gain, source, ids, slots, gates), (HBM, out_grad)],
        [(VMEM, (ROWS, WIDE + FEAT), bf16), (VMEM, (ROWS, FEAT), bf16)],
        8,
        (0, 1000),
        scratch=(pltpu.VMEM((ROWS, FEAT), bf16), pltpu.SemaphoreType.DMA((2,))),
    )
    sent = exchange(rows)
    weights = [(HBM, w_gate), (HBM, w_up), (HBM, w_down)]
    sums = [*[(VMEM, (ROWS, HID), f32)] * 3, (VMEM, (ROWS, WIDE - FEAT), f32)]
    sibling = to_sibling(sent)
    early = local_call(
        own_blocks,
        [where, *held(sent, sibling), *weights],
        sums,
        8,
        (0, 1000),
        scratch=(
            pltpu.VMEM((2, FEAT, HID), bf16),
            pltpu.VMEM((2, FEAT, HID), bf16),
            pltpu.VMEM((2, HID, FEAT), bf16),
            pltpu.SemaphoreType.DMA((2, 3)),
        ),
    )
    later, *early = lax.optimization_barrier((sent, *early))
    first, second = to_place(sent, 1), to_place(later, 2)
    first, *early = lax.optimization_barrier((first, *early))
    across = to_place(first, 2)
    first_halves = [to_sibling(first[: ROWS // 2]), to_sibling(first[ROWS // 2 :])]
    early = local_call(
        first_block,
        [where, *held(first), *weights, *held(*early)],
        sums,
        8,
        (0, 1000),
        scratch=(
            pltpu.VMEM((1, FEAT, HID), bf16),
            pltpu.VMEM((1, FEAT, HID), bf16),
            pltpu.VMEM((1, HID, FEAT), bf16),
            pltpu.SemaphoreType.DMA((3,)),
        ),
    )
    second, *early = lax.optimization_barrier((second, *early))
    second_halves = [to_sibling(second[: ROWS // 2]), to_sibling(second[ROWS // 2 :])]
    near = [sent, first, second]
    near_sibling = [sibling, *first_halves, *second_halves]
    gate, up, hid, mean = local_call(
        next_blocks,
        [where, *held(*first_halves, second, *second_halves, *early, w_gate, w_up, w_down)],
        sums,
        4,
        (10**9, 1000),
    )
    across, mean = lax.optimization_barrier((across, mean))
    across_sibling = to_sibling(across)
    act, d_gate, d_up, tail, across_other = local_call(
        last_blocks,
        [where, *held(across, across_sibling, gate, up, hid, mean, w_down, w_gate, w_up)],
        [
            *[(VMEM, (ROWS, HID), bf16)] * 3,
            (VMEM, (ROWS, WIDE - FEAT), bf16),
            (VMEM, (ROWS, BOTH), bf16),
        ],
        4,
        (10**9, 1000),
    )
    term_inputs = [where, *held(act, d_gate, d_up, tail, w_down, w_gate, w_up)]
    across_own, second_other = local_call(own_across, term_inputs, [(VMEM, (ROWS, BOTH), bf16)] * 2, 4, (0, 1000))
    across_sum, later_tail = lax.optimization_barrier((joined(across_own, to_sibling(across_other)), tail))
    term_inputs[4] = (VMEM, later_tail)
    other, own = [
        local_call(functools.partial(near_terms, side), term_inputs, [(VMEM, (ROWS, BOTH), bf16)] * n, 4, (0, 1000))
        for side, n in ((1, 2), (0, 3))
    ]
    theirs = [to_sibling(value) for value in (*other, second_other)]
    blocks = [(HBM, block) for block in (*near, across, *near_sibling, across_sibling)]
    home_sums = [joined(mine, term) for mine, term in zip(own, theirs)] + [across_sum]
    home_sums, late_gates = sent_home(home_sums, gates)
    tables = local_call(
        route_tables,
        fetched(ids, slots, late_gates, source, gain),
        [
            (VMEM, (ROWS, ROWS), bf16),
            (VMEM, (3, ROWS, ROWS), bf16),
            (VMEM, (8, ROWS), jnp.int32),
            (VMEM, (8, ROWS), f32),
            (VMEM, (1, FEAT), f32),
        ],
        4,
        (0, 1000),
    )
    grads = local_call(
        weight_grads,
        [where, *blocks, *fetched(act, d_gate, d_up)],
        [(HBM, (1, D, HID), bf16), (HBM, (1, D, HID), bf16), (HBM, (1, HID, D), bf16)],
        20,
        (2 * 3 * 2 * ROWS * D * HID, 22 * 10**6),
        scratch=(
            pltpu.VMEM((8, ROWS, BOTH), bf16),
            pltpu.VMEM((8, FEAT, HID), bf16),
            pltpu.VMEM((8, FEAT, HID), bf16),
            pltpu.VMEM((8, HID, FEAT), bf16),
            pltpu.SemaphoreType.DMA((10,)),
            pltpu.SemaphoreType.DMA((8, 3)),
        ),
    )
    home_sums, tables, grads = lax.optimization_barrier((home_sums, tables, grads))
    home = exchange(home_sums)
    moe, grad_hidden, grad_gates = local_call(
        finish,
        held(home, kept, *tables),
        [(COPY, (ROWS, FEAT), bf16), (COPY, (ROWS, FEAT), bf16), (COPY, (8, ROWS), f32)],
        4,
        (0, 1000),
    )
    return (moe, grad_hidden, grad_gates.T, *grads)


def solution(mesh):
    split = Mesh(mesh.devices.reshape(4, 2, 4, 4), ("y", "core", "x", "z"))
    heads, seq = ("y", "core"), ("x", "z")
    return jax.shard_map(
        on_device,
        mesh=split,
        in_specs=(
            P(seq, heads),
            P(heads),
            P(seq),
            P(seq, None),
            P(seq, None),
            P(seq, None),
            P(seq, None, heads),
            P(seq, None, heads),
            P(seq, heads, None),
            P(seq, heads),
        ),
        out_specs=(
            P(seq, heads),
            P(seq, heads),
            P(seq, None),
            P(seq, None, heads),
            P(seq, None, heads),
            P(seq, heads, None),
        ),
        check_vma=False,
    )
```

```python
import functools

import jax
import jax.numpy as jnp
from jax import lax
from jax.experimental import pallas as pl
from jax.experimental.pallas import tpu as pltpu
from jax.sharding import Mesh, PartitionSpec as P

D = 7168
CAP = 8
ROWS = 128
FEAT = 896
WIDE = 1024
BOTH = WIDE + FEAT
HID = 256
EPSILON = 1e-06
PLACES = ((0, 1, 3, 2), (0, 3, 1, 2))

f32 = jnp.float32
bf16 = jnp.bfloat16
SMEM, VMEM, COPY, HBM = "smem", "vmem", "copy", "hbm"


def nn(a, b):
    return lax.dot_general(a, b, (((1,), (0,)), ((), ())), preferred_element_type=f32)


def nt(a, b):
    return lax.dot_general(a, b, (((1,), (1,)), ((), ())), preferred_element_type=f32)


def tn(a, b):
    return lax.dot_general(a, b, (((0,), (0,)), ((), ())), preferred_element_type=f32)


def local_call(kernel, inputs, outputs, mib, cost, scratch=()):
    in_specs, args = [], []
    for kind, value in inputs:
        space = {SMEM: pltpu.SMEM, HBM: pl.ANY}.get(kind, pltpu.VMEM)
        in_specs.append(pl.BlockSpec(memory_space=space))
        if kind != SMEM:
            value = pltpu.with_memory_space_constraint(value, pltpu.VMEM if kind == VMEM else pltpu.HBM)
        args.append(value)
    out_shape, out_specs = [], []
    for kind, shape, dtype in outputs:
        space = {VMEM: pltpu.VMEM, HBM: pltpu.HBM}.get(kind, jax.ShapeDtypeStruct)
        out_shape.append(space(shape, dtype))
        out_specs.append(pl.BlockSpec(memory_space=pl.ANY if kind == HBM else pltpu.VMEM))
    return pl.pallas_call(
        kernel,
        out_shape=out_shape,
        in_specs=in_specs,
        out_specs=out_specs,
        scratch_shapes=list(scratch),
        compiler_params=pltpu.CompilerParams(vmem_limit_bytes=mib * 2**20),
        cost_estimate=pl.CostEstimate(flops=cost[0], bytes_accessed=cost[1], transcendentals=0),
    )(*args)


def held(*values):
    return [(VMEM, value) for value in values]


def fetched(*values):
    return [(COPY, value) for value in values]


def split_two(value):
    high = value.astype(bf16)
    low = (value - high.astype(f32)).astype(bf16)
    return high, low


def slot_matches(ids, slots):
    live = (ids < 16) & (slots >= 0) & (slots < CAP)
    target = jnp.where(live, ids * CAP + slots, ROWS)
    slot = lax.broadcasted_iota(jnp.int32, (ROWS, ROWS), 0)
    return live, [slot == target[k : k + 1, :] for k in range(8)]


def pick_rows(matches, parent):
    pick = matches[0]
    for match in matches[1:]:
        pick = pick | match
    pick = jnp.where(pick, 1.0, 0.0).astype(bf16)
    row = lax.broadcasted_iota(jnp.int32, (ROWS, ROWS), 0)
    from_parent = jnp.where(row == parent, 1.0, 0.0).astype(bf16)
    return pick, nt(pick, from_parent).astype(bf16)


def mix_of(matches, gates):
    mix = jnp.zeros((ROWS, ROWS), f32)
    for k, match in enumerate(matches):
        mix = mix + jnp.where(match, gates[k : k + 1, :], 0.0)
    return mix


def prepare(hidden, gain, source, ids, slots, gates, cotangent, rows, kept):
    _, matches = slot_matches(ids[...], slots[...])
    pick, select = pick_rows(matches, source[...] & (ROWS - 1))
    gate = jnp.sum(mix_of(matches, gates[...]), axis=1, keepdims=True)
    beam = nn(select, hidden[...])
    rows[:, :FEAT] = (beam * gain[...][None, :]).astype(bf16)
    square = jnp.sum(beam * beam, axis=1, keepdims=True) * (1.0 / D)
    high, low = split_two(square)
    lane = lax.broadcasted_iota(jnp.int32, (ROWS, WIDE - FEAT), 1)
    tail = jnp.where(lane == 0, high.astype(f32), jnp.where(lane == 1, low.astype(f32), 0.0))
    rows[:, FEAT:WIDE] = tail.astype(bf16)
    rows[:, WIDE:] = (nn(pick, cotangent[...]) * gate).astype(bf16)
    kept[...] = hidden[...]


def heads_here():
    y, core = lax.axis_index("y"), lax.axis_index("core")
    heads = []
    for side in (core, 1 - core):
        heads += [(y ^ jnp.where(side == 0, PLACES[0][i], PLACES[1][i])) * 2 + side for i in range(4)]
    return jnp.stack(heads).astype(jnp.int32)


def head_at(heads, place, side):
    return heads[4 * side + place]


def row_part(head):
    return pl.ds(pl.multiple_of(head * FEAT, FEAT), FEAT)


def column_part(head):
    return pl.ds(pl.multiple_of(head * FEAT, 128), FEAT)


def weight_copies(where, side, place, weights, targets, sems):
    head = head_at(where, place, side)
    w_gate, w_up, w_down = weights
    sources = (w_gate.at[0, row_part(head), :], w_up.at[0, row_part(head), :], w_down.at[0, :, column_part(head)])
    copies = [pltpu.make_async_copy(*pair, sems.at[j]) for j, pair in enumerate(zip(sources, targets))]
    for copy in copies:
        copy.start()
    return copies


def add_blocks(copies, blocks, parts, totals, squares):
    gate, up, hid = totals
    for n, block in enumerate(blocks):
        squares = squares + block[:, FEAT:WIDE].astype(f32)
        for copy in copies[n]:
            copy.wait()
        gate = gate + nn(block[:, :FEAT], parts[0][n])
        up = up + nn(block[:, :FEAT], parts[1][n])
        hid = hid + nt(block[:, WIDE:], parts[2][n])
    return (gate, up, hid), squares


def own_blocks(where, own, sibling, w_gate, w_up, w_down, *refs):
    gate, up, hid, mean, *parts, sems = refs
    weights = (w_gate, w_up, w_down)
    copies = [weight_copies(where, side, 0, weights, [p.at[side] for p in parts], sems.at[side]) for side in range(2)]
    zero = jnp.zeros((ROWS, HID), f32)
    squares = jnp.zeros((ROWS, WIDE - FEAT), f32)
    totals, squares = add_blocks(copies, (own, sibling), parts, (zero, zero, zero), squares)
    gate[...], up[...], hid[...] = totals
    mean[...] = squares


def first_block(where, own, w_gate, w_up, w_down, *refs):
    sums, results, (*parts, sems) = refs[:4], refs[4:8], refs[8:]
    copies = [weight_copies(where, 0, 1, (w_gate, w_up, w_down), [p.at[0] for p in parts], sems)]
    totals, squares = add_blocks(copies, (own,), parts, [ref[...] for ref in sums[:3]], sums[3][...])
    results[0][...], results[1][...], results[2][...] = totals
    results[3][...] = squares


def next_blocks(where, first_low, first_high, second, second_low, second_high, *refs):
    sums, (w_gate, w_up, w_down), results = refs[:4], refs[4:7], refs[7:]
    first_sibling = jnp.concatenate([first_low[...], first_high[...]], axis=0)
    second_sibling = jnp.concatenate([second_low[...], second_high[...]], axis=0)
    totals, squares = [ref[...] for ref in sums[:3]], sums[3][...]
    for place, side, block in ((1, 1, first_sibling), (2, 0, second), (2, 1, second_sibling)):
        head = head_at(where, place, side)
        rows, columns = row_part(head), column_part(head)
        parts = ([w_gate[0, rows, :]], [w_up[0, rows, :]], [w_down[0, :, columns]])
        totals, squares = add_blocks(((),), (block,), parts, totals, squares)
    results[0][...], results[1][...], results[2][...] = totals
    results[3][...] = squares


def expert_terms(where, act, d_gate, d_up, w_down, w_gate, w_up, side, results, tail):
    for i in results:
        head = head_at(where, i, side)
        rows, columns = row_part(head), column_part(head)
        results[i][:, :FEAT] = nn(act, w_down[0, :, columns]).astype(bf16)
        term = nt(d_gate, w_gate[0, rows, :]) + nt(d_up, w_up[0, rows, :])
        results[i][:, FEAT : FEAT + FEAT] = term.astype(bf16)
        results[i][:, FEAT + FEAT :] = tail


def last_blocks(where, *refs):
    blocks, (first_gate, first_up, first_hid, mean), (w_down, w_gate, w_up) = refs[:2], refs[2:6], refs[6:9]
    act, grad_gate, grad_up, tail_out, across_other = refs[9:]
    gate, up, hid = first_gate[...], first_up[...], first_hid[...]
    squares = mean[...]
    for side, block in enumerate(blocks):
        squares = squares + block[:, FEAT:WIDE].astype(f32)
        head = head_at(where, 3, side)
        rows, columns = row_part(head), column_part(head)
        gate = gate + nn(block[:, :FEAT], w_gate[0, rows, :])
        up = up + nn(block[:, :FEAT], w_up[0, rows, :])
        hid = hid + nt(block[:, WIDE:], w_down[0, :, columns])
    inverse = lax.rsqrt(jnp.sum(squares, axis=1, keepdims=True) + EPSILON)
    gate = gate * inverse
    up = up * inverse
    sigmoid = jax.nn.sigmoid(gate)
    hidden_act = (gate * sigmoid * up).astype(bf16)
    score = jnp.sum(hidden_act.astype(f32) * hid, axis=1, keepdims=True)
    scaled = hid * inverse
    d_gate = (scaled * up * sigmoid * (1.0 + gate * (1.0 - sigmoid))).astype(bf16)
    d_up = (scaled * gate * sigmoid).astype(bf16)
    act[...] = hidden_act
    grad_gate[...] = d_gate
    grad_up[...] = d_up
    dot = jnp.sum(d_gate.astype(f32) * gate + d_up.astype(f32) * up, axis=1, keepdims=True)
    dot = dot * inverse * (1.0 / D)
    lane = lax.broadcasted_iota(jnp.int32, (ROWS, WIDE - FEAT), 1)
    me = 2 * head_at(where, 0, 0)
    tail = jnp.zeros((ROWS, WIDE - FEAT), f32)
    for base, value in ((0, score), (64, dot)):
        high, low = split_two(value)
        tail = jnp.where(lane == base + me, high.astype(f32), tail)
        tail = jnp.where(lane == base + me + 1, low.astype(f32), tail)
    tail = tail.astype(bf16)
    tail_out[...] = tail
    expert_terms(where, hidden_act, d_gate, d_up, w_down, w_gate, w_up, 1, {3: across_other}, tail)


def own_across(where, act, grad_gate, grad_up, tail, w_down, w_gate, w_up, across, second_other):
    terms = (where, act[...], grad_gate[...], grad_up[...], w_down, w_gate, w_up)
    expert_terms(*terms, 0, {3: across}, tail[...])
    expert_terms(*terms, 1, {2: second_other}, tail[...])


def near_terms(side, where, act, grad_gate, grad_up, tail, w_down, w_gate, w_up, *terms):
    results = {i: terms[i] for i in reversed(range(len(terms)))}
    expert_terms(where, act[...], grad_gate[...], grad_up[...], w_down, w_gate, w_up, side, results, tail[...])


def weight_grads(where, *refs):
    blocks, (act, grad_gate, grad_up, out_gate, out_up, out_down) = refs[:10], refs[10:16]
    held_rows, buf_gate, buf_up, buf_down, load_sems, store_sems = refs[16:]
    loads = [[] for _ in range(8)]
    for i, block in enumerate(blocks):
        n = i if i < 5 else (i + 5) // 2 if i < 9 else 7
        start = ROWS // 2 if i in (6, 8) else 0
        rows = slice(start, start + block.shape[0])
        loads[n].append(pltpu.make_async_copy(block, held_rows.at[n, rows, :], load_sems.at[i]))
        loads[n][-1].start()
    act_t = act[...].T
    stores = []
    for n in range(8):
        for load in loads[n]:
            load.wait()
        head = head_at(where, n % 4, n // 4)
        beam_t = held_rows[n, :, :FEAT].T
        for j, (left, right, buf, target) in enumerate(
            (
                (act_t, held_rows[n, :, WIDE:], buf_down, out_down.at[0, :, column_part(head)]),
                (beam_t, grad_gate[...], buf_gate, out_gate.at[0, row_part(head), :]),
                (beam_t, grad_up[...], buf_up, out_up.at[0, row_part(head), :]),
            )
        ):
            buf[n] = nn(left, right).astype(bf16)
            stores.append(pltpu.make_async_copy(buf.at[n], target, store_sems.at[n, j]))
            stores[-1].start()
    for store in stores:
        store.wait()


def route_tables(ids, slots, gates, source, gain, select, mix, targets, kept_gates, kept_gain):
    live, matches = slot_matches(ids[...], slots[...])
    select[...] = pick_rows(matches, source[...] & (ROWS - 1))[1]
    rest = mix_of(matches, gates[...])
    for i in range(3):
        mix[i] = rest.astype(bf16)
        rest = rest - mix[i].astype(f32)
    targets[...] = jnp.where(live, ids[...] * CAP + slots[...], ROWS)
    kept_gates[...] = gates[...]
    kept_gain[...] = gain[...][None, :]


def finish(home, hidden, select, mix, targets, gates, gain, moe, grad_hidden, grad_gates):
    rows = home[:, :FEAT]
    moe[...] = (tn(mix[0], rows) + (tn(mix[1], rows) + tn(mix[2], rows))).astype(bf16)
    tail = home[:, FEAT + FEAT :].astype(f32)
    lane = lax.broadcasted_iota(jnp.int32, tail.shape, 1)
    score = jnp.sum(jnp.where(lane < 64, tail, 0.0), axis=1, keepdims=True)
    dot = jnp.sum(jnp.where(lane < 64, 0.0, tail), axis=1, keepdims=True)
    slot = lax.broadcasted_iota(jnp.int32, (ROWS, ROWS), 0)
    found = [
        jnp.sum(jnp.where(slot == targets[k : k + 1, :], score, 0.0), axis=0, keepdims=True) for k in range(8)
    ]
    found = jnp.concatenate(found, axis=0)
    grad_gates[...] = jnp.where(targets[...] < ROWS, found / gates[...], 0.0)
    picks = select[...]
    back = tn(picks, home[:, FEAT : FEAT + FEAT]) * gain[...]
    dots = jnp.where(picks.astype(f32) > 0, dot, 0.0)
    per_parent = jnp.sum(dots.T, axis=1, keepdims=True)
    grad_hidden[...] = (back - hidden[...].astype(f32) * per_parent).astype(bf16)


def to_place(values, place):
    pairs = [(2 * y + core, 2 * (y ^ PLACES[core][place]) + core) for y in range(4) for core in range(2)]
    return lax.ppermute(values, ("y", "core"), pairs)


def to_sibling(values):
    return lax.ppermute(values, "core", [(0, 1), (1, 0)])


def sent_home(sums, beside):
    mine, first, second, across = sums
    passing, beside = lax.optimization_barrier((to_place(across, 2), beside))
    first = joined(first, passing)
    return joined(mine, to_place(first, 1), to_place(second, 2)), beside


def joined(*parts):
    total = parts[0].astype(f32)
    for part in parts[1:]:
        total = total + part.astype(f32)
    return total.astype(bf16)


def exchange(rows):
    width = rows.shape[1]
    pieces = rows.reshape(16, CAP, width)
    return lax.all_to_all(pieces, ("x", "z"), 0, 0, tiled=True).reshape(ROWS, width)


def on_device(
    hidden, norm_gain, beam_src, route_ids, route_slots, route_gates, w_gate, w_up, w_down, out_grad
):
    where = (SMEM, heads_here())
    gain = norm_gain
    source = beam_src.reshape(1, ROWS)
    ids, slots, gates = route_ids.T, route_slots.T, route_gates.T
    rows, kept = local_call(
        prepare,
        fetched(hidden, gain, source, ids, slots, gates, out_grad),
        [(VMEM, (ROWS, WIDE + FEAT), bf16), (VMEM, (ROWS, FEAT), bf16)],
        8,
        (0, 1000),
    )
    sent = exchange(rows)
    weights = [(HBM, w_gate), (HBM, w_up), (HBM, w_down)]
    sums = [*[(VMEM, (ROWS, HID), f32)] * 3, (VMEM, (ROWS, WIDE - FEAT), f32)]
    sibling = to_sibling(sent)
    early = local_call(
        own_blocks,
        [where, *held(sent, sibling), *weights],
        sums,
        8,
        (0, 1000),
        scratch=(
            pltpu.VMEM((2, FEAT, HID), bf16),
            pltpu.VMEM((2, FEAT, HID), bf16),
            pltpu.VMEM((2, HID, FEAT), bf16),
            pltpu.SemaphoreType.DMA((2, 3)),
        ),
    )
    later, *early = lax.optimization_barrier((sent, *early))
    first, second = to_place(sent, 1), to_place(later, 2)
    first, *early = lax.optimization_barrier((first, *early))
    across = to_place(first, 2)
    first_halves = [to_sibling(first[: ROWS // 2]), to_sibling(first[ROWS // 2 :])]
    early = local_call(
        first_block,
        [where, *held(first), *weights, *held(*early)],
        sums,
        8,
        (0, 1000),
        scratch=(
            pltpu.VMEM((1, FEAT, HID), bf16),
            pltpu.VMEM((1, FEAT, HID), bf16),
            pltpu.VMEM((1, HID, FEAT), bf16),
            pltpu.SemaphoreType.DMA((3,)),
        ),
    )
    second, *early = lax.optimization_barrier((second, *early))
    second_halves = [to_sibling(second[: ROWS // 2]), to_sibling(second[ROWS // 2 :])]
    near = [sent, first, second]
    near_sibling = [sibling, *first_halves, *second_halves]
    gate, up, hid, mean = local_call(
        next_blocks,
        [where, *held(*first_halves, second, *second_halves, *early, w_gate, w_up, w_down)],
        sums,
        4,
        (10**9, 1000),
    )
    across, mean = lax.optimization_barrier((across, mean))
    across_sibling = to_sibling(across)
    act, d_gate, d_up, tail, across_other = local_call(
        last_blocks,
        [where, *held(across, across_sibling, gate, up, hid, mean, w_down, w_gate, w_up)],
        [
            *[(VMEM, (ROWS, HID), bf16)] * 3,
            (VMEM, (ROWS, WIDE - FEAT), bf16),
            (VMEM, (ROWS, BOTH), bf16),
        ],
        4,
        (10**9, 1000),
    )
    term_inputs = [where, *held(act, d_gate, d_up, tail, w_down, w_gate, w_up)]
    across_own, second_other = local_call(own_across, term_inputs, [(VMEM, (ROWS, BOTH), bf16)] * 2, 4, (0, 1000))
    across_sum, later_tail = lax.optimization_barrier((joined(across_own, to_sibling(across_other)), tail))
    term_inputs[4] = (VMEM, later_tail)
    other, own = [
        local_call(functools.partial(near_terms, side), term_inputs, [(VMEM, (ROWS, BOTH), bf16)] * n, 4, (0, 1000))
        for side, n in ((1, 2), (0, 3))
    ]
    theirs = [to_sibling(value) for value in (*other, second_other)]
    blocks = [(HBM, block) for block in (*near, across, *near_sibling, across_sibling)]
    home_sums = [joined(mine, term) for mine, term in zip(own, theirs)] + [across_sum]
    home_sums[2], late_gates = lax.optimization_barrier((home_sums[2], gates))
    tables = local_call(
        route_tables,
        fetched(ids, slots, late_gates, source, gain),
        [
            (VMEM, (ROWS, ROWS), bf16),
            (VMEM, (3, ROWS, ROWS), bf16),
            (VMEM, (8, ROWS), jnp.int32),
            (VMEM, (8, ROWS), f32),
            (VMEM, (1, FEAT), f32),
        ],
        4,
        (0, 1000),
    )
    home_sums, tables = sent_home(home_sums, tables)
    grads = local_call(
        weight_grads,
        [where, *blocks, *fetched(act, d_gate, d_up)],
        [(HBM, (1, D, HID), bf16), (HBM, (1, D, HID), bf16), (HBM, (1, HID, D), bf16)],
        20,
        (2 * 3 * 2 * ROWS * D * HID, 22 * 10**6),
        scratch=(
            pltpu.VMEM((8, ROWS, BOTH), bf16),
            pltpu.VMEM((8, FEAT, HID), bf16),
            pltpu.VMEM((8, FEAT, HID), bf16),
            pltpu.VMEM((8, HID, FEAT), bf16),
            pltpu.SemaphoreType.DMA((10,)),
            pltpu.SemaphoreType.DMA((8, 3)),
        ),
    )
    home_sums, *grads = lax.optimization_barrier((home_sums, *grads))
    home = exchange(home_sums)
    moe, grad_hidden, grad_gates = local_call(
        finish,
        held(home, kept, *tables),
        [(COPY, (ROWS, FEAT), bf16), (COPY, (ROWS, FEAT), bf16), (COPY, (8, ROWS), f32)],
        4,
        (0, 1000),
    )
    return (moe, grad_hidden, grad_gates.T, *grads)


def solution(mesh):
    split = Mesh(mesh.devices.reshape(4, 2, 4, 4), ("y", "core", "x", "z"))
    heads, seq = ("y", "core"), ("x", "z")
    return jax.shard_map(
        on_device,
        mesh=split,
        in_specs=(
            P(seq, heads),
            P(heads),
            P(seq),
            P(seq, None),
            P(seq, None),
            P(seq, None),
            P(seq, None, heads),
            P(seq, None, heads),
            P(seq, heads, None),
            P(seq, heads),
        ),
        out_specs=(
            P(seq, heads),
            P(seq, heads),
            P(seq, None),
            P(seq, None, heads),
            P(seq, None, heads),
            P(seq, heads, None),
        ),
        check_vma=False,
    )
```
